32 devices in a mesh: grp: 4 (over x, core), row: 2 (over y), col: 4 (over z).
Axes of the slice: x: 2, y: 2, z: 4, core: 2. Of those that a mesh axis runs over, the one named last changes fastest.
Arguments:
- velocity: float32 [3, 4, 1024, 1024], P(None, 'col', ('grp', 'row')), may hold values from -8 to 8
- profile: int32 [4], P('col'), may hold values from 0 to 1
- x_filters: bfloat16 [2, 1024, 1024], replicated, may hold values from 0 to 1
- z_filter: bfloat16 [1024, 1024], replicated, may hold values from 0 to 1
Outputs:
- stress: float32 [6, 4, 1024, 1024], P(None, 'col', ('grp', 'row'))
The draws below stay inside these ranges and needn't reach their ends.
All inputs are finite; a program needn't handle non-finite values.
Results may differ from the reference program's by a relative error of at most 0.0031.
Values may be sent and summed in bfloat16 or wider, within the bound.
No kernel may reach another device: no remote copies, remote signals or barrier semaphores. Data moves between devices by JAX's collectives and lax.ppermute only.
A program may use at most 64 MiB of HBM per device.

```python
import math
import jax
import jax.numpy as jnp
from jax import lax

NX = 1024
NZ = 1024
PROFILES = 2
NY = 4


def filter_stack(key, extent_cells, stack_count):
    width_key, jitter_key = jax.random.split(key)
    narrow = 8.0
    widest = 0.5 * extent_cells
    widths = jnp.exp(jax.random.uniform(width_key, (stack_count, extent_cells, 1), jnp.float32, math.log(narrow), math.log(widest)))
    position = jnp.arange(extent_cells, dtype=jnp.float32)
    distance = jnp.abs(position[:, None] - position[None, :])
    distance = jnp.minimum(distance, extent_cells - distance)
    kernel = jnp.exp(-0.5 * (distance / widths) ** 2) / (2.5066283 * widths)
    jitter = 0.3 * jnp.clip(jax.random.normal(jitter_key, (stack_count, extent_cells, extent_cells), jnp.float32), -1.5, 1.5)
    return 0.5 * jnp.eye(extent_cells, dtype=jnp.float32) + 0.5 * kernel * (1.0 + jitter)


def draw_x_filters(key, part):
    return filter_stack(jax.random.fold_in(key, 3), NX, PROFILES).astype(jnp.bfloat16)


def draw_z_filter(key, part):
    return filter_stack(jax.random.fold_in(key, 7), NZ, 1)[0].astype(jnp.bfloat16)


def plant(drawn, rng, least, largest):
    shape = drawn.shape
    place = [jax.random.randint(jax.random.fold_in(rng, axis), (), 0, shape[axis]) for axis in range(len(shape))]
    drawn = drawn.at[tuple(place)].set(least)
    longest = shape.index(max(shape))
    place[longest] = (place[longest] + 1) % shape[longest]
    return drawn.at[tuple(place)].set(largest)


def shard_levels(own_key, shape, pieces, least, top_value):
    factor_of, own = 1.0, jax.random.fold_in(own_key, 6)
    for axis_at, parts in pieces:
        steps = jnp.exp(jax.random.uniform(jax.random.fold_in(own, axis_at), (parts,), jnp.float32, least / len(pieces), top_value / len(pieces)))
        factor_of = factor_of * jnp.repeat(steps, shape[axis_at] // parts).reshape([-1 if axis == axis_at else 1 for axis in range(len(shape))])
    return factor_of


def noise(own_key, dims, deviation, reach, cuts=(), kind=jnp.bfloat16):
    factor_of = shard_levels(own_key, dims, cuts, -0.22, 0.18) if cuts else 1.0
    values = jax.random.normal(own_key, dims, jnp.float32) * deviation * factor_of
    return jnp.minimum(jnp.maximum(values, -reach), reach).astype(kind)


def setup_inputs(seed: int = 0) -> dict:
    key_list = jax.random.split(jax.random.key(seed), 5)
    velocity = noise(key_list[0], (3, NY, NZ, NX), 2.0, 8.0, ((1, 4), (2, 8)), jnp.float32)
    profile = plant(jax.random.randint(key_list[1], (NY,), 0, PROFILES), jax.random.fold_in(key_list[1], 1), 0, PROFILES - 1).astype(jnp.int32)
    x_filters = draw_x_filters(jax.random.fold_in(key_list[4], 71), 0)
    z_filter = draw_z_filter(jax.random.fold_in(key_list[4], 71), 0)
    return dict(velocity=velocity, profile=profile, x_filters=x_filters, z_filter=z_filter)


STEP_SIZE = 0.25
VISCOSITY = 0.8
PRODUCT_PAIRS = ((0, 0), (0, 1), (0, 2), (1, 1), (1, 2), (2, 2))


def row_rate(window):
    center = window[:, 1]
    y_next = window[:, 2]
    y_prev = window[:, 0]
    z_next = jnp.roll(center, -1, axis=1)
    z_prev = jnp.roll(center, 1, axis=1)
    x_next = jnp.roll(center, -1, axis=2)
    x_prev = jnp.roll(center, 1, axis=2)
    advect = center[0] * (0.5 * (x_next - x_prev)) + center[1] * (0.5 * (y_next - y_prev)) + center[2] * (0.5 * (z_next - z_prev))
    laplace = x_next + x_prev + y_next + y_prev + z_next + z_prev - 6.0 * center
    return VISCOSITY * laplace - advect


def velocity_rate(values):
    padded = jnp.pad(values, ((0, 0), (1, 1), (0, 0), (0, 0)))

    def one_row(row_number):
        return row_rate(lax.dynamic_slice_in_dim(padded, row_number, 3, 1))

    stacked = lax.map(one_row, jnp.arange(values.shape[1], dtype=jnp.int32))
    return jnp.transpose(stacked, (1, 0, 2, 3))


def reference(velocity, profile, x_filters, z_filter):
    section_one = velocity + STEP_SIZE * velocity_rate(velocity)
    section_two = 0.75 * velocity + 0.25 * (section_one + STEP_SIZE * velocity_rate(section_one))
    advanced = velocity / 3.0 + (2.0 / 3.0) * (section_two + STEP_SIZE * velocity_rate(section_two))

    def analyse(row_number):
        planes = lax.dynamic_index_in_dim(advanced, row_number, 1, keepdims=False)
        components = [planes[0], planes[1], planes[2]] + [planes[left_comp] * planes[right_comp] for left_comp, right_comp in PRODUCT_PAIRS]
        fields = jnp.stack(components).astype(jnp.bfloat16)
        matrix = lax.dynamic_index_in_dim(x_filters, profile[row_number], 0, keepdims=False)
        x_pass = jnp.einsum("ox,fzx->foz", matrix.astype(jnp.float32), fields.astype(jnp.float32)).astype(jnp.bfloat16)
        z_pass = jnp.einsum("fos,rs->for", x_pass.astype(jnp.float32), z_filter.astype(jnp.float32))
        return jnp.stack([z_pass[3 + number] - z_pass[left_comp] * z_pass[right_comp] for number, (left_comp, right_comp) in enumerate(PRODUCT_PAIRS)])

    stress = lax.map(analyse, jnp.arange(velocity.shape[1], dtype=jnp.int32))
    return jnp.transpose(stress, (1, 0, 2, 3))
```

```python
import functools

import jax
import jax.numpy as jnp
from jax import lax
from jax.experimental import pallas as pl
from jax.experimental.pallas import tpu as pltpu
from jax.sharding import PartitionSpec as P

STEP_SIZE = 0.25
VISCOSITY = 0.8
PRODUCT_PAIRS = ((0, 0), (0, 1), (0, 2), (1, 1), (1, 2), (2, 2))

PLANE = ("grp", "row")
WIRE = jnp.bfloat16
CHUNKS = ((0,), (1,), (2,))
CHIPS = (0, 1, 4, 5)
HALO = 8
VMEM_BYTES = 56 * 1024 * 1024
NT = (((1,), (1,)), ((), ()))


def exchange(value, axis, flip):
    count = lax.axis_size(axis)
    return lax.ppermute(value, axis, [(i, i ^ flip) for i in range(count)])


def whole(memory=pltpu.VMEM):
    return pl.BlockSpec(memory_space=memory)


def step_kernel(slabs, q_ref, *refs):
    mains, halos = refs[:4], refs[4:8]
    outs, (start, one, two) = refs[8:-3], refs[-3:]
    q = q_ref[0]
    rows = mains[0].shape[-2]
    width = mains[0].shape[-1]
    for buffer in (start, one, two):
        buffer[0] = jnp.zeros(buffer.shape[1:], buffer.dtype)
        buffer[slabs + 1] = jnp.zeros(buffer.shape[1:], buffer.dtype)
    for flip in range(slabs):
        y = (q ^ flip) + 1
        halo = halos[flip][...].astype(jnp.float32)
        start[y, :, 0:HALO] = halo
        start[y, :, HALO : HALO + rows] = mains[flip][...].reshape(3, rows, width).astype(jnp.float32)
        start[y, :, HALO + rows :] = halo

    last = HALO + rows

    def rates(src, y, row):
        above, below = (row, row) if row else (0, last)
        here = [src[y, comp, row : row + HALO] for comp in range(3)]
        half = [0.5 * value for value in here]
        result = []
        for comp in range(3):
            center = here[comp]
            y_next, y_prev = src[y + 1, comp, row : row + HALO], src[y - 1, comp, row : row + HALO]
            z_next = src[y, comp, above + 1 : above + 1 + HALO]
            z_prev = src[y, comp, below - 1 : below - 1 + HALO]
            x_next = pltpu.roll(center, width - 1, 1)
            x_prev = pltpu.roll(center, 1, 1)
            advect = half[0] * (x_next - x_prev) + half[1] * (y_next - y_prev) + half[2] * (z_next - z_prev)
            laplace = (x_next + x_prev) + (y_next + y_prev) + (z_next + z_prev) - 6.0 * center
            result.append((center, VISCOSITY * laplace - advect))
        return result

    def put(buffer, y, comp, row, value):
        buffer[y, comp, row : row + HALO] = value
        if row == 0:
            buffer[y, comp, last : last + HALO] = value

    def section_one(number, carry):
        y = number + 1
        for row in range(0, last, HALO):
            for comp, (center, rate) in enumerate(rates(start, y, row)):
                put(one, y, comp, row, center + STEP_SIZE * rate)
        return carry

    def section_two(number, carry):
        y = number + 1
        for row in range(0, last, HALO):
            for comp, (center, rate) in enumerate(rates(one, y, row)):
                base = start[y, comp, row : row + HALO]
                put(two, y, comp, row, 0.75 * base + 0.25 * (center + STEP_SIZE * rate))
        return carry

    lax.fori_loop(0, slabs, section_one, 0)
    lax.fori_loop(0, slabs, section_two, 0)
    for flip in range(slabs):
        y = (q ^ flip) + 1
        for row in range(HALO, last, 2 * HALO):
            pair = [rates(two, y, row), rates(two, y, row + HALO)]
            for number, comps in enumerate(CHUNKS):
                out = outs[number * slabs + flip]
                for place, comp in enumerate(comps):
                    values = []
                    for part in range(2):
                        at = row + part * HALO
                        center, rate = pair[part][comp]
                        base = start[y, comp, at : at + HALO]
                        values.append(base * (1.0 / 3.0) + (2.0 / 3.0) * (center + STEP_SIZE * rate))
                    out[place, row - HALO : row + HALO] = jnp.concatenate(values, 0).astype(out.dtype)


def advance(velocity, profile):
    slabs = lax.axis_size("col")
    q = lax.axis_index("col")
    v = velocity[:, 0]
    block, width = v.shape[1:]
    rows = block // slabs
    narrow = v.astype(WIRE)
    plane = lax.axis_size(PLANE)
    tail = lax.ppermute(narrow[:, block - HALO :], PLANE, [(i, (i + 1) % plane) for i in range(plane)])
    head = lax.ppermute(narrow[:, :HALO], PLANE, [((i + 1) % plane, i) for i in range(plane)])
    mains = [v]
    for flip in range(1, slabs):
        mains.append(exchange(lax.dynamic_slice_in_dim(narrow, rows * (q ^ flip), rows, 1), "col", flip))
    framed = jnp.concatenate([tail, narrow, head], axis=1)
    first = lax.broadcasted_iota(jnp.int32, (3, HALO, width), 1) < HALO // 2
    halos = []
    for flip in range(slabs):
        at = rows * (q ^ flip)
        before = lax.dynamic_slice_in_dim(framed, at, HALO, 1)
        after = lax.dynamic_slice_in_dim(framed, at + rows + HALO, HALO, 1)
        halo = jnp.where(first, after, before)
        halos.append(exchange(halo, "col", flip) if flip else halo)

    grid_spec = pltpu.PrefetchScalarGridSpec(
        num_scalar_prefetch=1,
        grid=(1,),
        in_specs=[pl.BlockSpec((3, rows, width), lambda i, q_ref: (0, q_ref[0], 0))] + [whole()] * 7,
        out_specs=[whole()] * (len(CHUNKS) * slabs),
        scratch_shapes=[pltpu.VMEM((slabs + 2, 3, rows + 2 * HALO, width), jnp.float32)] * 3,
    )
    cells = 3 * slabs * rows * width
    pieces = pl.pallas_call(
        functools.partial(step_kernel, slabs),
        out_shape=[
            jax.ShapeDtypeStruct((len(comps), rows, width), WIRE) for comps in CHUNKS for _ in range(slabs)
        ],
        grid_spec=grid_spec,
        compiler_params=pltpu.CompilerParams(vmem_limit_bytes=VMEM_BYTES),
        cost_estimate=pl.CostEstimate(flops=75 * cells, bytes_accessed=6 * cells, transcendentals=0),
        name="advance",
    )(q.reshape(1).astype(jnp.int32), *mains, *halos)
    chunks = []
    for number in range(len(CHUNKS)):
        mine = pieces[number * slabs : (number + 1) * slabs]
        chunks.append([mine[0]] + [exchange(mine[flip], "col", flip) for flip in range(1, slabs)])
    return chunks


def fields_of(comps):
    singles = list(comps)
    pairs = [(a, b) for b in comps for a in range(b + 1)]
    return singles, pairs


def x_kernel(number, slabs, place_ref, matrices, *refs):
    inputs = refs[: 2 * (number + 1)]
    outs = refs[2 * (number + 1) : -4]
    matrix, cells, fields, sem = refs[-4:]
    q, me, prof = place_ref[0], place_ref[1], place_ref[2]
    core = (me // 2) % 2
    copies = []
    for slot, flip in enumerate(CHIPS):
        copies.append(
            pltpu.make_async_copy(
                matrices.at[prof, pl.ds(pl.multiple_of((me ^ flip) * 128, 128), 128)],
                matrix.at[pl.ds(slot * 128, 128)],
                sem.at[slot],
            )
        )
        copies[-1].start()
    for chunk in range(number + 1):
        for other in range(2):
            ref = inputs[2 * chunk + other]
            rows = ref.shape[2]
            base = 128 * (core ^ other)
            for flip in range(slabs):
                at = pl.multiple_of(base + rows * (q ^ flip), rows)
                for place, comp in enumerate(CHUNKS[chunk]):
                    cells[comp, pl.ds(at, rows)] = ref[flip, place]
    singles, pairs = fields_of(CHUNKS[number])
    for at, (a, b) in enumerate(pairs):
        product = cells[a].astype(jnp.float32) * cells[b].astype(jnp.float32)
        fields[at] = product.astype(jnp.bfloat16)
    for copy in copies:
        copy.wait()
    for at in range(len(singles) + len(pairs)):
        field = cells[singles[at]] if at < len(singles) else fields[at - len(singles)]
        result = lax.dot_general(matrix[...], field, NT, preferred_element_type=jnp.float32)
        for slot in range(len(CHIPS)):
            outs[slot][at] = result[slot * 128 : (slot + 1) * 128].astype(jnp.bfloat16)


def z_kernel(number, place_ref, z_filter, *refs):
    singles, pairs = fields_of(CHUNKS[number])
    count = len(singles) + len(pairs)
    blocks = refs[: len(CHIPS)]
    earlier = refs[len(CHIPS) : len(CHIPS) + number]
    keep, stress, lines, passed, made, sem = refs[-6:]
    me = place_ref[0]
    for slot, flip in enumerate(CHIPS):
        for core in range(2):
            source = ((me ^ flip) & ~2) | (2 * core)
            lane = pl.multiple_of(128 * source, 128)
            for at in range(count):
                lines[at * 128 : (at + 1) * 128, pl.ds(lane, 128)] = blocks[slot][at, :, 128 * core : 128 * core + 128]
    passed[...] = lax.dot_general(lines[...], z_filter[...], NT, preferred_element_type=jnp.float32)
    means = {}
    for chunk in range(number):
        for place, comp in enumerate(CHUNKS[chunk]):
            means[comp] = earlier[chunk][place]
    for place, comp in enumerate(singles):
        means[comp] = passed[place * 128 : (place + 1) * 128]
        keep[place] = means[comp]
    copies = []
    for at, pair in enumerate(pairs):
        row = (len(singles) + at) * 128
        made[at] = passed[row : row + 128] - means[pair[0]] * means[pair[1]]
        copies.append(
            pltpu.make_async_copy(made.at[at], stress.at[PRODUCT_PAIRS.index(pair), 0], sem.at[at])
        )
        copies[-1].start()
    for copy in copies:
        copy.wait()


def fast_body(velocity, profile, x_filters, z_filter):
    width = velocity.shape[3]
    slabs = lax.axis_size("col")
    q = lax.axis_index("col").astype(jnp.int32)
    me = lax.axis_index(PLANE).astype(jnp.int32)
    place = jnp.stack([q, me, profile[0]])
    chunks = advance(velocity, profile)
    gathered, means, stress = [], [], None
    for number, pieces in enumerate(chunks):
        mine = jnp.stack(pieces)
        gathered += [mine, exchange(mine, "grp", 1)]
        singles, pairs = fields_of(CHUNKS[number])
        count = len(singles) + len(pairs)
        blocks = pl.pallas_call(
            functools.partial(x_kernel, number, slabs),
            out_shape=[jax.ShapeDtypeStruct((count, 128, 256), jnp.bfloat16)] * len(CHIPS),
            in_specs=[whole(pltpu.SMEM), whole(pl.ANY)] + [whole()] * len(gathered),
            out_specs=[whole()] * len(CHIPS),
            scratch_shapes=[
                pltpu.VMEM((512, width), jnp.bfloat16),
                pltpu.VMEM((3, 256, width), jnp.bfloat16),
                pltpu.VMEM((len(pairs), 256, width), jnp.bfloat16),
                pltpu.SemaphoreType.DMA((len(CHIPS),)),
            ],
            compiler_params=pltpu.CompilerParams(vmem_limit_bytes=VMEM_BYTES),
            cost_estimate=pl.CostEstimate(
                flops=2 * 512 * width * 256 * count, bytes_accessed=2 * 1024 * width, transcendentals=0
            ),
            name=f"x_filter_{number}",
        )(place, x_filters, *gathered)
        blocks = [blocks[0]] + [exchange(blocks[slot], PLANE, CHIPS[slot]) for slot in range(1, len(CHIPS))]
        extra = [] if stress is None else [stress]
        keep, stress = pl.pallas_call(
            functools.partial(z_kernel, number),
            out_shape=[
                jax.ShapeDtypeStruct((len(singles), 128, width), jnp.float32),
                jax.ShapeDtypeStruct((6, 1, 128, width), jnp.float32),
            ],
            in_specs=[whole(pltpu.SMEM)] + [whole()] * (1 + len(CHIPS) + len(means)) + [whole(pl.ANY)] * len(extra),
            out_specs=[whole(), whole(pl.ANY)],
            input_output_aliases={2 + len(CHIPS) + len(means): 1} if extra else {},
            scratch_shapes=[
                pltpu.VMEM((count * 128, width), jnp.bfloat16),
                pltpu.VMEM((count * 128, width), jnp.float32),
                pltpu.VMEM((len(pairs), 128, width), jnp.float32),
                pltpu.SemaphoreType.DMA((len(pairs),)),
            ],
            compiler_params=pltpu.CompilerParams(vmem_limit_bytes=VMEM_BYTES),
            cost_estimate=pl.CostEstimate(
                flops=2 * 128 * count * width * width, bytes_accessed=4 * 1024 * width, transcendentals=0
            ),
            name=f"z_filter_{number}",
        )(me.reshape(1), z_filter, *blocks, *means, *extra)
        means.append(keep)
    return stress


def extended(cells, sides, width):
    for axis, dim in sides:
        count = lax.axis_size(axis)
        head = lax.slice_in_dim(cells, 0, width, axis=dim)
        tail = lax.slice_in_dim(cells, cells.shape[dim] - width, cells.shape[dim], axis=dim)
        cells = jnp.concatenate(
            [
                lax.ppermute(tail, axis, [(i, (i + 1) % count) for i in range(count)]),
                cells,
                lax.ppermute(head, axis, [((i + 1) % count, i) for i in range(count)]),
            ],
            axis=dim,
        )
    return cells


def wall_zero(padded, extent, y_rows):
    height = padded.shape[1]
    all_rows = y_rows * lax.axis_size("col")
    row_index = lax.axis_index("col") * y_rows + jnp.arange(height, dtype=jnp.int32) - extent
    inside = (row_index >= 0) & (row_index < all_rows)
    return padded * inside.astype(padded.dtype)[None, :, None, None]


def shrink_rate(padded):
    center = padded[:, 1:-1, 1:-1]
    y_next = padded[:, 2:, 1:-1]
    y_prev = padded[:, :-2, 1:-1]
    z_next = padded[:, 1:-1, 2:]
    z_prev = padded[:, 1:-1, :-2]
    x_next = jnp.roll(center, -1, axis=3)
    x_prev = jnp.roll(center, 1, axis=3)
    advect = (
        center[0] * (0.5 * (x_next - x_prev))
        + center[1] * (0.5 * (y_next - y_prev))
        + center[2] * (0.5 * (z_next - z_prev))
    )
    laplace = x_next + x_prev + y_next + y_prev + z_next + z_prev - 6.0 * center
    return VISCOSITY * laplace - advect


def z_apply(received, z_filter):
    return jnp.einsum("fyos,rs->fyor", received, z_filter, preferred_element_type=jnp.float32)


def body(velocity, profile, x_filters, z_filter):
    y_rows = velocity.shape[1]

    def extend(current):
        padded = extended(current, ((("grp", "row"), 2), ("col", 1)), 1)
        return wall_zero(padded, 1, y_rows)

    section_one = velocity + STEP_SIZE * shrink_rate(extend(velocity))
    section_two = 0.75 * velocity + 0.25 * (
        section_one + STEP_SIZE * shrink_rate(extend(section_one))
    )
    advanced = velocity / 3.0 + 2.0 / 3.0 * (
        section_two + STEP_SIZE * shrink_rate(extend(section_two))
    )
    components = [advanced[0], advanced[1], advanced[2]] + [
        advanced[left_comp] * advanced[right_comp] for left_comp, right_comp in PRODUCT_PAIRS
    ]
    fields = jnp.stack(components).astype(jnp.bfloat16)
    matrices = jnp.take(x_filters, profile, axis=0)
    x_pass = jnp.einsum(
        "yox,fyzx->fyoz", matrices, fields, preferred_element_type=jnp.float32
    ).astype(jnp.bfloat16)
    filtered = z_apply(
        lax.all_to_all(x_pass, ("grp", "row"), split_axis=2, concat_axis=3, tiled=True), z_filter
    )
    stress = jnp.stack(
        [
            filtered[3 + number] - filtered[left_comp] * filtered[right_comp]
            for number, (left_comp, right_comp) in enumerate(PRODUCT_PAIRS)
        ]
    )
    return stress


def solution(mesh):
    placed = (P(None, "col", ("grp", "row"), None), P("col"), P(), P())

    def run(velocity, profile, x_filters, z_filter):
        shape = dict(mesh.shape)
        plane = shape["grp"] * shape["row"]
        suits = (
            (shape["grp"], shape["row"], shape["col"]) == (4, 2, 4)
            and velocity.shape == (3, shape["col"], 128 * plane, 1024)
            and x_filters.shape[1:] == z_filter.shape == (1024, 1024)
        )
        return jax.shard_map(
            fast_body if suits else body,
            mesh=mesh,
            in_specs=placed,
            out_specs=P(None, "col", ("grp", "row"), None),
            check_vma=False,
        )(velocity, profile, x_filters, z_filter)

    return run
```

```python
import functools

import jax
import jax.numpy as jnp
from jax import lax
from jax.experimental import pallas as pl
from jax.experimental.pallas import tpu as pltpu
from jax.sharding import PartitionSpec as P

STEP_SIZE = 0.25
VISCOSITY = 0.8
PRODUCT_PAIRS = ((0, 0), (0, 1), (0, 2), (1, 1), (1, 2), (2, 2))
FIELDS = 3 + len(PRODUCT_PAIRS)

PLANE = ("grp", "row")
WIRE = jnp.bfloat16
CHUNKS = ((0,), (1, 2), (3,))
CHIPS = (0, 1, 4, 5)
HALO = 8
REACH = 3
VMEM_BYTES = 32 * 1024 * 1024
NT = (((1,), (1,)), ((), ()))
TN = (((0,), (0,)), ((), ()))
TAIL_PARTS = 2
WAITED = 3
COSTS = dict(prepare=3.0, advance=5.0, x_filter_0=0.1, x_filter_1=0.1, x_filter_2=0.1, x_filter_3=0.1, z_filter_first=0.1, z_filter_last=0.1)


def cost(name):
    return pl.CostEstimate(flops=0, bytes_accessed=int(3.7e6 * COSTS[name]), transcendentals=0)


def exchange(value, axis, flip):
    count = lax.axis_size(axis)
    return lax.ppermute(value, axis, [(i, i ^ flip) for i in range(count)])


def delayed(value, *earlier):
    return lax.optimization_barrier((value, earlier))[0]


def whole(memory=pltpu.VMEM):
    return pl.BlockSpec(memory_space=memory)


def prepare_kernel(slabs, place_ref, x_filters, z_filter, rows_out, *refs):
    lines_out, (sem,) = refs[: len(CHUNKS)], refs[len(CHUNKS) :]
    q, me, prof = place_ref[0], place_ref[1], place_ref[2]
    copies = []
    for slot, flip in enumerate(CHIPS):
        at = pl.multiple_of((me ^ flip) * 128, 128)
        copies.append(
            pltpu.make_async_copy(
                x_filters.at[prof, pl.ds(at, 128)], rows_out.at[pl.ds(slot * 128, 128)], sem.at[slot]
            )
        )
        copies[-1].start()
    rows = 128 // slabs
    picks = []
    for flips in CHUNKS:
        per_core = rows * len(flips)
        target = lax.broadcasted_iota(jnp.int32, (2 * per_core, 256), 0)
        source = lax.broadcasted_iota(jnp.int32, (2 * per_core, 256), 1)
        core, inner = target // per_core, target % per_core
        wanted = core * 128 + rows * (q ^ (flips[0] + inner // rows)) + inner % rows
        picks.append((source == wanted).astype(jnp.bfloat16))
    pick = jnp.concatenate(picks, axis=0)
    for slot, flip in enumerate(CHIPS):
        low = (me ^ flip) & ~2
        pair = jnp.concatenate(
            [z_filter[:, pl.ds(pl.multiple_of(128 * (low + 2 * core), 128), 128)] for core in range(2)], axis=1
        )
        picked = lax.dot_general(pick, pair, NT, preferred_element_type=jnp.float32).astype(jnp.bfloat16)
        at = 0
        for number, flips in enumerate(CHUNKS):
            cells = 2 * rows * len(flips)
            lines_out[number][slot * cells : (slot + 1) * cells] = picked[at : at + cells]
            at += cells
    for copy in copies:
        copy.wait()


def step_kernel(slabs, q_ref, *refs):
    mains, halos = refs[:slabs], refs[slabs : 2 * slabs]
    outs, (start, one, two, done) = refs[2 * slabs : -4], refs[-4:]
    q = q_ref[0]
    rows, width = outs[0].shape[-2:]
    parts = width // 128
    for buffer in (start, one, two):
        buffer[0] = jnp.zeros(buffer.shape[1:], buffer.dtype)
        buffer[slabs + 1] = jnp.zeros(buffer.shape[1:], buffer.dtype)
    for flip in range(slabs):
        y = (q ^ flip) + 1
        for comp in range(3):
            for row in range(0, rows, 16):
                block = mains[flip][comp, row : row + 16].astype(jnp.float32)
                for half in range(2):
                    for part in range(parts):
                        at = (REACH + row + 8 * half) * 8 + part
                        start[y, comp, pl.ds(at, 8, stride=8)] = block[
                            8 * half : 8 * half + 8, 128 * part : 128 * part + 128
                        ]
            halo = halos[flip][comp].astype(jnp.float32)
            for part in range(parts):
                lanes = halo[:, 128 * part : 128 * part + 128]
                start[y, comp, pl.ds((REACH + rows) * 8 + part, REACH, stride=8)] = lanes[:REACH]
                start[y, comp, pl.ds(part, REACH, stride=8)] = lanes[HALO - REACH :]

    lane = lax.broadcasted_iota(jnp.int32, (8, 128), 1)
    at_end, at_start = lane == 127, lane == 0

    def sweep(src, y, first, count, emit):
        behind = [src[y, comp, 8 * first - 8 : 8 * first] for comp in range(3)]
        here = [src[y, comp, 8 * first : 8 * first + 8] for comp in range(3)]
        for row in range(first, first + count):
            ahead = [src[y, comp, 8 * row + 8 : 8 * row + 16] for comp in range(3)]
            lower, upper = [], []
            for comp in range(3):
                drift = (0.5 * STEP_SIZE) * here[comp]
                upper.append(STEP_SIZE * VISCOSITY - drift)
                lower.append(STEP_SIZE * VISCOSITY + drift)
            for comp in range(3):
                center = here[comp]
                next_lane = pltpu.roll(center, 127, 1)
                x_next = jnp.where(at_end, pltpu.roll(next_lane, 7, 0), next_lane)
                prev_lane = pltpu.roll(center, 1, 1)
                x_prev = jnp.where(at_start, pltpu.roll(prev_lane, 1, 0), prev_lane)
                y_next = src[y + 1, comp, 8 * row : 8 * row + 8]
                y_prev = src[y - 1, comp, 8 * row : 8 * row + 8]
                along_x = upper[0] * x_next + lower[0] * x_prev
                along_y = upper[1] * y_next + lower[1] * y_prev
                along_z = upper[2] * ahead[comp] + lower[2] * behind[comp]
                rest = (1.0 - 6.0 * STEP_SIZE * VISCOSITY) * center
                emit(row, comp, (along_x + along_y) + (along_z + rest))
            behind, here = here, ahead

    def section_one(number, carry):
        y = number + 1

        def emit(row, comp, moved):
            one[y, comp, 8 * row : 8 * row + 8] = moved

        sweep(start, y, 1, rows + 2 * REACH - 2, emit)
        return carry

    def section_two(number, carry):
        y = number + 1

        def emit(row, comp, moved):
            at = slice(8 * row, 8 * row + 8)
            two[y, comp, at] = 0.75 * start[y, comp, at] + 0.25 * moved

        sweep(one, y, 2, rows + 2 * REACH - 4, emit)
        return carry

    def section_three(number, carry):
        y = number + 1

        def emit(row, comp, moved):
            at = slice(8 * row, 8 * row + 8)
            to = slice(8 * (row - REACH), 8 * (row - REACH) + 8)
            done[number, comp, to] = (1.0 / 3.0) * start[y, comp, at] + (2.0 / 3.0) * moved

        sweep(two, y, REACH, rows, emit)
        return carry

    lax.fori_loop(0, slabs, section_one, 0)
    lax.fori_loop(0, slabs, section_two, 0)
    lax.fori_loop(0, slabs, section_three, 0)
    for flip in range(slabs):
        for comp in range(3):
            for row in range(0, rows, 16):
                for part in range(parts):
                    pair = [done[q ^ flip, comp, pl.ds((row + at) * 8 + part, 8, stride=8)] for at in (0, 8)]
                    outs[flip][comp, row : row + 16, 128 * part : 128 * part + 128] = jnp.concatenate(
                        pair, axis=0
                    ).astype(outs[flip].dtype)


def advance(velocity, filters):
    slabs, plane = lax.axis_size("col"), lax.axis_size(PLANE)
    q = lax.axis_index("col").astype(jnp.int32)
    v = velocity[:, 0]
    block, width = v.shape[1:]
    rows = block // slabs
    narrow = v.astype(WIRE)
    tail = lax.ppermute(narrow[:, block - HALO :], PLANE, [(j, (j + 1) % plane) for j in range(plane)])
    head = lax.ppermute(narrow[:, :HALO], PLANE, [((j + 1) % plane, j) for j in range(plane)])
    mains = [lax.dynamic_slice_in_dim(v, rows * q, rows, 1)]
    for flip in range(1, slabs):
        mains.append(exchange(lax.dynamic_slice_in_dim(narrow, rows * (q ^ flip), rows, 1), "col", flip))
    low = lax.broadcasted_iota(jnp.int32, (3, HALO, width), 1) < HALO // 2
    halos = []
    for flip in range(slabs):
        at = rows * (q ^ flip)
        before = lax.dynamic_slice_in_dim(narrow, jnp.maximum(at - HALO, 0), HALO, 1)
        after = lax.dynamic_slice_in_dim(narrow, jnp.minimum(at + rows, block - HALO), HALO, 1)
        before = jnp.where(at == 0, tail, before)
        after = jnp.where(at == block - rows, head, after)
        halos.append(jnp.where(low, after, before))
    halos[1], mains[1] = lax.optimization_barrier((halos[1], mains[1]))
    for flip in (3, 2, 1):
        halos[flip] = exchange(halos[flip], "col", flip)
    mains, halos, filters = lax.optimization_barrier((mains, halos, filters))

    lines = 8 * (rows + 2 * REACH)
    pieces = pl.pallas_call(
        functools.partial(step_kernel, slabs),
        out_shape=[jax.ShapeDtypeStruct((3, rows, width), WIRE)] * slabs,
        in_specs=[whole(pltpu.SMEM)] + [whole()] * (2 * slabs),
        out_specs=[whole()] * slabs,
        scratch_shapes=[pltpu.VMEM((slabs + 2, 3, lines, 128), jnp.float32)] * 3
        + [pltpu.VMEM((slabs, 3, 8 * rows, 128), jnp.float32)],
        compiler_params=pltpu.CompilerParams(vmem_limit_bytes=VMEM_BYTES),
        cost_estimate=cost("advance"),
        name="advance",
    )(q.reshape(1), *mains, *halos)
    pieces = list(pieces)
    pieces[1], pieces[2] = exchange(pieces[1], "col", 1), exchange(pieces[2], "col", 2)
    pieces[3] = exchange(pieces[3], "col", 3)
    return pieces, filters


def x_kernel(place_ref, matrix, *refs):
    inputs, outs, (fields,) = refs[: -len(CHIPS) - 1], refs[-len(CHIPS) - 1 : -1], refs[-1:]
    core = (place_ref[1] // 2) % 2
    half = len(inputs) // 2
    for other in range(2):
        for piece in range(half):
            ref = inputs[other * half + piece]
            rows = ref.shape[1]
            at = pl.multiple_of(rows * (half * (core ^ other) + piece), rows)
            for comp in range(3):
                fields[comp, pl.ds(at, rows)] = ref[comp]
            for number, (a, b) in enumerate(PRODUCT_PAIRS):
                product = ref[a].astype(jnp.float32) * ref[b].astype(jnp.float32)
                fields[3 + number, pl.ds(at, rows)] = product.astype(jnp.bfloat16)
    cells = fields.shape[1]
    group = fields[...].reshape(FIELDS * cells, fields.shape[2])
    result = lax.dot_general(group, matrix[...], NT, preferred_element_type=jnp.float32)
    for number in range(FIELDS):
        for slot in range(len(CHIPS)):
            part = result[number * cells : (number + 1) * cells, slot * 128 : (slot + 1) * 128]
            outs[slot][number] = part.astype(jnp.bfloat16)


def z_sum(lines, blocks, columns):
    left = jnp.concatenate(
        [jnp.concatenate([block[number] for number in range(FIELDS)], axis=1) for block in blocks], axis=0
    )
    right = jnp.concatenate([line[:, columns] for line in lines], axis=0)
    return lax.dot_general(left, right, TN, preferred_element_type=jnp.float32)


def z_first_kernel(*refs):
    count = (len(refs) - 1) // (1 + len(CHIPS))
    lines, blocks, passed = refs[:count], refs[count:-1], refs[-1]
    passed[...] = z_sum(lines, blocks, slice(None)).reshape(passed.shape)


def z_last_kernel(passed, lines, *refs):
    blocks, (stress, made, sem) = refs[: len(CHIPS)], refs[len(CHIPS) :]
    copies = []
    width = passed.shape[2] // TAIL_PARTS
    for part in range(TAIL_PARTS):
        columns = slice(part * width, (part + 1) * width)
        result = z_sum([lines], blocks, columns)
        total = [passed[at, :, columns] + result[at * 128 : (at + 1) * 128] for at in range(FIELDS)]
        for at, (a, b) in enumerate(PRODUCT_PAIRS):
            made[at, :, columns] = total[3 + at] - total[a] * total[b]
        copies.append(pltpu.make_async_copy(made.at[:, :, columns], stress.at[:, 0, :, columns], sem.at[part]))
        copies[-1].start()
    for copy in copies:
        copy.wait()


def fast_body(velocity, profile, x_filters, z_filter):
    width = velocity.shape[3]
    slabs = lax.axis_size("col")
    q = lax.axis_index("col").astype(jnp.int32)
    me = lax.axis_index(PLANE).astype(jnp.int32)
    place = jnp.stack([q, me, profile[0]])
    params = pltpu.CompilerParams(vmem_limit_bytes=VMEM_BYTES)
    sizes = [2 * len(flips) * 128 // slabs for flips in CHUNKS]
    matrix, *lines = pl.pallas_call(
        functools.partial(prepare_kernel, slabs),
        out_shape=[jax.ShapeDtypeStruct((128 * len(CHIPS), width), jnp.bfloat16)]
        + [jax.ShapeDtypeStruct((len(CHIPS) * cells, z_filter.shape[0]), jnp.bfloat16) for cells in sizes],
        in_specs=[whole(pltpu.SMEM), whole(pl.ANY), whole()],
        out_specs=[whole()] * (1 + len(CHUNKS)),
        scratch_shapes=[pltpu.SemaphoreType.DMA((len(CHIPS),))],
        compiler_params=params,
        cost_estimate=cost("prepare"),
        name="prepare",
    )(place, x_filters, z_filter)

    pieces, (matrix, *lines) = advance(velocity, (matrix, *lines))
    blocks = []
    for number, flips in enumerate(CHUNKS):
        mine = [pieces[flip] for flip in flips]
        theirs = [exchange(piece, "grp", 1) for piece in mine]
        cells = sizes[number]
        made = pl.pallas_call(
            x_kernel,
            out_shape=[jax.ShapeDtypeStruct((FIELDS, cells, 128), jnp.bfloat16)] * len(CHIPS),
            in_specs=[whole(pltpu.SMEM)] + [whole()] * (1 + 2 * len(flips)),
            out_specs=[whole()] * len(CHIPS),
            scratch_shapes=[pltpu.VMEM((FIELDS, cells, width), jnp.bfloat16)],
            compiler_params=params,
            cost_estimate=cost(f"x_filter_{number}"),
            name=f"x_filter_{number}",
        )(place, matrix, *mine, *theirs)
        made = list(made)
        if number == len(CHUNKS) - 1:
            made = delayed(made, *blocks[-1][1:WAITED])
        if number == 1:
            made[3] = delayed(made[3], pieces[3])
        blocks.append([made[0]] + [exchange(made[slot], PLANE, CHIPS[slot]) for slot in range(1, len(CHIPS))])
        if number == 0:
            for flip in CHUNKS[1]:
                pieces[flip] = delayed(pieces[flip], *blocks[0][1:])
    early = len(CHUNKS) - 1
    passed = pl.pallas_call(
        z_first_kernel,
        out_shape=jax.ShapeDtypeStruct((FIELDS, 128, width), jnp.float32),
        in_specs=[whole()] * (early * (1 + len(CHIPS))),
        out_specs=whole(),
        compiler_params=params,
        cost_estimate=cost("z_filter_first"),
        name="z_filter_first",
    )(*lines[:early], *[block for sent in blocks[:early] for block in sent])
    return pl.pallas_call(
        z_last_kernel,
        out_shape=jax.ShapeDtypeStruct((len(PRODUCT_PAIRS), 1, 128, width), jnp.float32),
        in_specs=[whole()] * (2 + len(CHIPS)),
        out_specs=whole(pl.ANY),
        scratch_shapes=[
            pltpu.VMEM((len(PRODUCT_PAIRS), 128, width), jnp.float32),
            pltpu.SemaphoreType.DMA((TAIL_PARTS,)),
        ],
        compiler_params=params,
        cost_estimate=cost("z_filter_last"),
        name="z_filter_last",
    )(passed, lines[-1], *blocks[-1])


def extended(cells, sides, width):
    for axis, dim in sides:
        count = lax.axis_size(axis)
        head = lax.slice_in_dim(cells, 0, width, axis=dim)
        tail = lax.slice_in_dim(cells, cells.shape[dim] - width, cells.shape[dim], axis=dim)
        cells = jnp.concatenate(
            [
                lax.ppermute(tail, axis, [(i, (i + 1) % count) for i in range(count)]),
                cells,
                lax.ppermute(head, axis, [((i + 1) % count, i) for i in range(count)]),
            ],
            axis=dim,
        )
    return cells


def wall_zero(padded, extent, y_rows):
    height = padded.shape[1]
    all_rows = y_rows * lax.axis_size("col")
    row_index = lax.axis_index("col") * y_rows + jnp.arange(height, dtype=jnp.int32) - extent
    inside = (row_index >= 0) & (row_index < all_rows)
    return padded * inside.astype(padded.dtype)[None, :, None, None]


def shrink_rate(padded):
    center = padded[:, 1:-1, 1:-1]
    y_next = padded[:, 2:, 1:-1]
    y_prev = padded[:, :-2, 1:-1]
    z_next = padded[:, 1:-1, 2:]
    z_prev = padded[:, 1:-1, :-2]
    x_next = jnp.roll(center, -1, axis=3)
    x_prev = jnp.roll(center, 1, axis=3)
    advect = (
        center[0] * (0.5 * (x_next - x_prev))
        + center[1] * (0.5 * (y_next - y_prev))
        + center[2] * (0.5 * (z_next - z_prev))
    )
    laplace = x_next + x_prev + y_next + y_prev + z_next + z_prev - 6.0 * center
    return VISCOSITY * laplace - advect


def z_apply(received, z_filter):
    return jnp.einsum("fyos,rs->fyor", received, z_filter, preferred_element_type=jnp.float32)


def body(velocity, profile, x_filters, z_filter):
    y_rows = velocity.shape[1]

    def extend(current):
        padded = extended(current, ((("grp", "row"), 2), ("col", 1)), 1)
        return wall_zero(padded, 1, y_rows)

    section_one = velocity + STEP_SIZE * shrink_rate(extend(velocity))
    section_two = 0.75 * velocity + 0.25 * (
        section_one + STEP_SIZE * shrink_rate(extend(section_one))
    )
    advanced = velocity / 3.0 + 2.0 / 3.0 * (
        section_two + STEP_SIZE * shrink_rate(extend(section_two))
    )
    components = [advanced[0], advanced[1], advanced[2]] + [
        advanced[left_comp] * advanced[right_comp] for left_comp, right_comp in PRODUCT_PAIRS
    ]
    fields = jnp.stack(components).astype(jnp.bfloat16)
    matrices = jnp.take(x_filters, profile, axis=0)
    x_pass = jnp.einsum(
        "yox,fyzx->fyoz", matrices, fields, preferred_element_type=jnp.float32
    ).astype(jnp.bfloat16)
    filtered = z_apply(
        lax.all_to_all(x_pass, ("grp", "row"), split_axis=2, concat_axis=3, tiled=True), z_filter
    )
    stress = jnp.stack(
        [
            filtered[3 + number] - filtered[left_comp] * filtered[right_comp]
            for number, (left_comp, right_comp) in enumerate(PRODUCT_PAIRS)
        ]
    )
    return stress


def solution(mesh):
    placed = (P(None, "col", ("grp", "row"), None), P("col"), P(), P())

    def run(velocity, profile, x_filters, z_filter):
        shape = dict(mesh.shape)
        plane = shape["grp"] * shape["row"]
        suits = (
            (shape["grp"], shape["row"], shape["col"]) == (4, 2, 4)
            and velocity.shape == (3, shape["col"], 128 * plane, 1024)
            and x_filters.shape[1:] == z_filter.shape == (1024, 1024)
        )
        return jax.shard_map(
            fast_body if suits else body,
            mesh=mesh,
            in_specs=placed,
            out_specs=P(None, "col", ("grp", "row"), None),
            check_vma=False,
        )(velocity, profile, x_filters, z_filter)

    return run
```

```python
import functools

import jax
import jax.numpy as jnp
from jax import lax
from jax.experimental import pallas as pl
from jax.experimental.pallas import tpu as pltpu
from jax.sharding import PartitionSpec as P

STEP_SIZE = 0.25
VISCOSITY = 0.8
PRODUCT_PAIRS = ((0, 0), (0, 1), (0, 2), (1, 1), (1, 2), (2, 2))
FIELDS = 3 + len(PRODUCT_PAIRS)

PLANE = ("grp", "row")
WIRE = jnp.bfloat16
CHUNKS = ((0,), (1, 2), (3,))
CHIPS = (0, 1, 4, 5)
HALO = 8
REACH = 3
VMEM_BYTES = 32 * 1024 * 1024
NT = (((1,), (1,)), ((), ()))
TN = (((0,), (0,)), ((), ()))
TAIL_PARTS = 2
WAITED = 3
COSTS = dict(prepare=3.0, advance=5.0, x_filter_0=0.1, x_filter_1=0.1, x_filter_2=0.1, x_filter_3=0.1, z_filter_first=0.1, z_filter_last=0.1)


def cost(name):
    return pl.CostEstimate(flops=0, bytes_accessed=int(3.7e6 * COSTS[name]), transcendentals=0)


def exchange(value, axis, flip):
    count = lax.axis_size(axis)
    return lax.ppermute(value, axis, [(i, i ^ flip) for i in range(count)])


def delayed(value, *earlier):
    return lax.optimization_barrier((value, earlier))[0]


def whole(memory=pltpu.VMEM):
    return pl.BlockSpec(memory_space=memory)


def prepare_kernel(slabs, place_ref, x_filters, z_filter, rows_out, *refs):
    lines_out, (sem,) = refs[: len(CHUNKS)], refs[len(CHUNKS) :]
    q, me, prof = place_ref[0], place_ref[1], place_ref[2]
    copies = []
    for core in range(2):
        for slot, flip in enumerate(CHIPS):
            at = pl.multiple_of((me ^ flip ^ (2 * core)) * 128, 128)
            to = (core * len(CHIPS) + slot) * 128
            copies.append(
                pltpu.make_async_copy(
                    x_filters.at[prof, pl.ds(at, 128)], rows_out.at[pl.ds(to, 128)], sem.at[core * len(CHIPS) + slot]
                )
            )
            copies[-1].start()
    rows = 128 // slabs
    target = lax.broadcasted_iota(jnp.int32, (128, 128), 0)
    source = lax.broadcasted_iota(jnp.int32, (128, 128), 1)
    pick = (source == rows * (q ^ (target // rows)) + target % rows).astype(jnp.bfloat16)
    for slot, flip in enumerate(CHIPS):
        for core in range(2):
            lanes = pl.ds(pl.multiple_of(128 * (me ^ flip ^ (2 * core)), 128), 128)
            picked = lax.dot_general(pick, z_filter[:, lanes], NT, preferred_element_type=jnp.float32)
            for number, flips in enumerate(CHUNKS):
                cells = rows * len(flips)
                part = picked[rows * flips[0] : rows * flips[0] + cells].astype(jnp.bfloat16)
                if number < len(CHUNKS) - 1:
                    at = (core * len(CHIPS) + slot) * cells
                else:
                    at = (slot * 2 + core) * cells
                lines_out[number][at : at + cells] = part
    for copy in copies:
        copy.wait()


def step_kernel(slabs, q_ref, *refs):
    mains, halos = refs[:slabs], refs[slabs : 2 * slabs]
    outs, (start, one, two, done) = refs[2 * slabs : -4], refs[-4:]
    q = q_ref[0]
    rows, width = outs[0].shape[-2:]
    parts = width // 128
    for buffer in (start, one, two):
        buffer[0] = jnp.zeros(buffer.shape[1:], buffer.dtype)
        buffer[slabs + 1] = jnp.zeros(buffer.shape[1:], buffer.dtype)
    for flip in range(slabs):
        y = (q ^ flip) + 1
        for comp in range(3):
            for row in range(0, rows, 16):
                block = mains[flip][comp, row : row + 16].astype(jnp.float32)
                for half in range(2):
                    for part in range(parts):
                        at = (REACH + row + 8 * half) * 8 + part
                        start[y, comp, pl.ds(at, 8, stride=8)] = block[
                            8 * half : 8 * half + 8, 128 * part : 128 * part + 128
                        ]
            halo = halos[flip][comp].astype(jnp.float32)
            for part in range(parts):
                lanes = halo[:, 128 * part : 128 * part + 128]
                start[y, comp, pl.ds((REACH + rows) * 8 + part, REACH, stride=8)] = lanes[:REACH]
                start[y, comp, pl.ds(part, REACH, stride=8)] = lanes[HALO - REACH :]

    lane = lax.broadcasted_iota(jnp.int32, (8, 128), 1)
    at_end, at_start = lane == 127, lane == 0

    def sweep(src, y, first, count, emit):
        behind = [src[y, comp, 8 * first - 8 : 8 * first] for comp in range(3)]
        here = [src[y, comp, 8 * first : 8 * first + 8] for comp in range(3)]
        for row in range(first, first + count):
            ahead = [src[y, comp, 8 * row + 8 : 8 * row + 16] for comp in range(3)]
            lower, upper = [], []
            for comp in range(3):
                drift = (0.5 * STEP_SIZE) * here[comp]
                upper.append(STEP_SIZE * VISCOSITY - drift)
                lower.append(STEP_SIZE * VISCOSITY + drift)
            for comp in range(3):
                center = here[comp]
                next_lane = pltpu.roll(center, 127, 1)
                x_next = jnp.where(at_end, pltpu.roll(next_lane, 7, 0), next_lane)
                prev_lane = pltpu.roll(center, 1, 1)
                x_prev = jnp.where(at_start, pltpu.roll(prev_lane, 1, 0), prev_lane)
                y_next = src[y + 1, comp, 8 * row : 8 * row + 8]
                y_prev = src[y - 1, comp, 8 * row : 8 * row + 8]
                along_x = upper[0] * x_next + lower[0] * x_prev
                along_y = upper[1] * y_next + lower[1] * y_prev
                along_z = upper[2] * ahead[comp] + lower[2] * behind[comp]
                rest = (1.0 - 6.0 * STEP_SIZE * VISCOSITY) * center
                emit(row, comp, (along_x + along_y) + (along_z + rest))
            behind, here = here, ahead

    def section_one(number, carry):
        y = number + 1

        def emit(row, comp, moved):
            one[y, comp, 8 * row : 8 * row + 8] = moved

        sweep(start, y, 1, rows + 2 * REACH - 2, emit)
        return carry

    def section_two(number, carry):
        y = number + 1

        def emit(row, comp, moved):
            at = slice(8 * row, 8 * row + 8)
            two[y, comp, at] = 0.75 * start[y, comp, at] + 0.25 * moved

        sweep(one, y, 2, rows + 2 * REACH - 4, emit)
        return carry

    def section_three(number, carry):
        y = number + 1

        def emit(row, comp, moved):
            at = slice(8 * row, 8 * row + 8)
            to = slice(8 * (row - REACH), 8 * (row - REACH) + 8)
            done[number, comp, to] = (1.0 / 3.0) * start[y, comp, at] + (2.0 / 3.0) * moved

        sweep(two, y, REACH, rows, emit)
        return carry

    lax.fori_loop(0, slabs, section_one, 0)
    lax.fori_loop(0, slabs, section_two, 0)
    lax.fori_loop(0, slabs, section_three, 0)
    for flip in range(slabs):
        for comp in range(3):
            for row in range(0, rows, 16):
                for part in range(parts):
                    pair = [done[q ^ flip, comp, pl.ds((row + at) * 8 + part, 8, stride=8)] for at in (0, 8)]
                    outs[flip][comp, row : row + 16, 128 * part : 128 * part + 128] = jnp.concatenate(
                        pair, axis=0
                    ).astype(outs[flip].dtype)


def advance(velocity, filters):
    slabs, plane = lax.axis_size("col"), lax.axis_size(PLANE)
    q = lax.axis_index("col").astype(jnp.int32)
    v = velocity[:, 0]
    block, width = v.shape[1:]
    rows = block // slabs
    tail = lax.ppermute(v[:, block - HALO :].astype(WIRE), PLANE, [(j, (j + 1) % plane) for j in range(plane)])
    head = lax.ppermute(v[:, :HALO].astype(WIRE), PLANE, [((j + 1) % plane, j) for j in range(plane)])
    mains = [lax.dynamic_slice_in_dim(v, rows * q, rows, 1)]
    for flip in range(1, slabs):
        mains.append(exchange(lax.dynamic_slice_in_dim(v, rows * (q ^ flip), rows, 1).astype(WIRE), "col", flip))
    low = lax.broadcasted_iota(jnp.int32, (3, HALO, width), 1) < HALO // 2
    halos = []
    for flip in range(slabs):
        at = rows * (q ^ flip)
        before = lax.dynamic_slice_in_dim(v, jnp.maximum(at - HALO, 0), HALO, 1).astype(WIRE)
        after = lax.dynamic_slice_in_dim(v, jnp.minimum(at + rows, block - HALO), HALO, 1).astype(WIRE)
        before = jnp.where(at == 0, tail, before)
        after = jnp.where(at == block - rows, head, after)
        halos.append(jnp.where(low, after, before))
    halos[1], mains[1] = lax.optimization_barrier((halos[1], mains[1]))
    for flip in (3, 2, 1):
        halos[flip] = exchange(halos[flip], "col", flip)
    mains, halos, filters = lax.optimization_barrier((mains, halos, filters))

    lines = 8 * (rows + 2 * REACH)
    pieces = pl.pallas_call(
        functools.partial(step_kernel, slabs),
        out_shape=[jax.ShapeDtypeStruct((3, rows, width), WIRE)] * slabs,
        in_specs=[whole(pltpu.SMEM)] + [whole()] * (2 * slabs),
        out_specs=[whole()] * slabs,
        scratch_shapes=[pltpu.VMEM((slabs + 2, 3, lines, 128), jnp.float32)] * 3
        + [pltpu.VMEM((slabs, 3, 8 * rows, 128), jnp.float32)],
        compiler_params=pltpu.CompilerParams(vmem_limit_bytes=VMEM_BYTES),
        cost_estimate=cost("advance"),
        name="advance",
    )(q.reshape(1), *mains, *halos)
    pieces = list(pieces)
    pieces[1], pieces[2] = exchange(pieces[1], "col", 1), exchange(pieces[2], "col", 2)
    pieces[3] = exchange(pieces[3], "col", 3)
    return pieces, filters


def x_kernel(cores, matrix, *refs):
    inputs, outs, (fields,) = refs[: -len(CHIPS) - 1], refs[-len(CHIPS) - 1 : -1], refs[-1:]
    cells = fields.shape[1]
    rows = cells // len(inputs)
    for piece, ref in enumerate(inputs):
        at = slice(rows * piece, rows * piece + rows)
        for comp in range(3):
            fields[comp, at] = ref[comp]
        for number, (a, b) in enumerate(PRODUCT_PAIRS):
            product = ref[a].astype(jnp.float32) * ref[b].astype(jnp.float32)
            fields[3 + number, at] = product.astype(jnp.bfloat16)
    group = fields[...].reshape(FIELDS * cells, fields.shape[2])
    result = lax.dot_general(
        group, matrix[: cores * len(CHIPS) * 128], NT, preferred_element_type=jnp.float32
    ).astype(jnp.bfloat16)
    for number in range(FIELDS):
        for core in range(cores):
            for slot in range(len(CHIPS)):
                at = (core * len(CHIPS) + slot) * 128
                outs[slot][core, number] = result[number * cells : (number + 1) * cells, at : at + 128]


def side_by_side(block):
    return jnp.concatenate([block[number] for number in range(FIELDS)], axis=1)


def z_sum(lines, blocks, columns):
    left = jnp.concatenate(blocks, axis=0)
    right = jnp.concatenate([line[:, columns] for line in lines], axis=0)
    return lax.dot_general(left, right, TN, preferred_element_type=jnp.float32)


def z_first_kernel(*refs):
    lines, first, others, second, passed = refs[:2], refs[2:6], refs[6], refs[7:11], refs[11]
    blocks = [side_by_side(ref[0]) for ref in first]
    blocks += [side_by_side(others[slot]) for slot in range(len(CHIPS))]
    blocks += [side_by_side(ref[0]) for ref in second]
    half = lines[1].shape[0] // 2
    passed[...] = z_sum([lines[0], lines[1].at[:half]], blocks, slice(None)).reshape(passed.shape)


def z_last_kernel(passed, line_second, line_last, others, *refs):
    blocks = [side_by_side(others[slot]) for slot in range(len(CHIPS))]
    blocks += [side_by_side(ref[0]) for ref in refs[: len(CHIPS)]]
    half = line_second.shape[0] // 2
    lines = [line_second.at[half:], line_last]
    stress, made, sem = refs[len(CHIPS) :]
    copies = []
    width = passed.shape[2] // TAIL_PARTS
    for part in range(TAIL_PARTS):
        columns = slice(part * width, (part + 1) * width)
        result = z_sum(lines, blocks, columns)
        total = [passed[at, :, columns] + result[at * 128 : (at + 1) * 128] for at in range(FIELDS)]
        for at, (a, b) in enumerate(PRODUCT_PAIRS):
            made[at, :, columns] = total[3 + at] - total[a] * total[b]
        copies.append(pltpu.make_async_copy(made.at[:, :, columns], stress.at[:, 0, :, columns], sem.at[part]))
        copies[-1].start()
    for copy in copies:
        copy.wait()


def fast_body(velocity, profile, x_filters, z_filter):
    width = velocity.shape[3]
    slabs = lax.axis_size("col")
    q = lax.axis_index("col").astype(jnp.int32)
    me = lax.axis_index(PLANE).astype(jnp.int32)
    place = jnp.stack([q, me, profile[0]])
    params = pltpu.CompilerParams(vmem_limit_bytes=VMEM_BYTES)
    sizes = [len(flips) * 128 // slabs for flips in CHUNKS]
    matrix, *lines = pl.pallas_call(
        functools.partial(prepare_kernel, slabs),
        out_shape=[jax.ShapeDtypeStruct((256 * len(CHIPS), width), jnp.bfloat16)]
        + [jax.ShapeDtypeStruct((2 * len(CHIPS) * cells, z_filter.shape[0]), jnp.bfloat16) for cells in sizes],
        in_specs=[whole(pltpu.SMEM), whole(pl.ANY), whole()],
        out_specs=[whole()] * (1 + len(CHUNKS)),
        scratch_shapes=[pltpu.SemaphoreType.DMA((2 * len(CHIPS),))],
        compiler_params=params,
        cost_estimate=cost("prepare"),
        name="prepare",
    )(place, x_filters, z_filter)

    pieces, (matrix, *lines) = advance(velocity, (matrix, *lines))

    def x_filter(number, cores, inputs):
        cells = sum(piece.shape[1] for piece in inputs)
        return list(
            pl.pallas_call(
                functools.partial(x_kernel, cores),
                out_shape=[jax.ShapeDtypeStruct((cores, FIELDS, cells, 128), jnp.bfloat16)] * len(CHIPS),
                in_specs=[whole()] * (1 + len(inputs)),
                out_specs=[whole()] * len(CHIPS),
                scratch_shapes=[pltpu.VMEM((FIELDS, cells, width), jnp.bfloat16)],
                compiler_params=params,
                cost_estimate=cost(f"x_filter_{number}"),
                name=f"x_filter_{number}",
            )(matrix, *inputs)
        )

    def to_chips(made):
        return [made[0]] + [exchange(made[slot], PLANE, CHIPS[slot]) for slot in range(1, len(CHIPS))]

    blocks = []
    for number, flips in enumerate(CHUNKS[:-1]):
        made = x_filter(number, 2, [pieces[flip] for flip in flips])
        if blocks:
            made = delayed(made, *blocks[-1][1 : len(CHIPS)])
        sent = to_chips(made)
        blocks.append(sent)
    mine = [pieces[flip] for flip in CHUNKS[-1]]
    made = x_filter(len(CHUNKS) - 1, 1, mine + [exchange(piece, "grp", 1) for piece in mine])
    made[3] = delayed(made[3], blocks[-1][1])
    last = to_chips(made)
    first, second = blocks
    first_others = exchange(jnp.stack([block[1] for block in first]), "grp", 1)
    passed = pl.pallas_call(
        z_first_kernel,
        out_shape=jax.ShapeDtypeStruct((FIELDS, 128, width), jnp.float32),
        in_specs=[whole()] * (3 + 2 * len(CHIPS)),
        out_specs=whole(),
        compiler_params=params,
        cost_estimate=cost("z_filter_first"),
        name="z_filter_first",
    )(*lines[:2], *first, first_others, *second)
    second_others = exchange(delayed(jnp.stack([block[1] for block in second]), passed, *last[1:]), "grp", 1)
    return pl.pallas_call(
        z_last_kernel,
        out_shape=jax.ShapeDtypeStruct((len(PRODUCT_PAIRS), 1, 128, width), jnp.float32),
        in_specs=[whole()] * (4 + len(CHIPS)),
        out_specs=whole(pl.ANY),
        scratch_shapes=[
            pltpu.VMEM((len(PRODUCT_PAIRS), 128, width), jnp.float32),
            pltpu.SemaphoreType.DMA((TAIL_PARTS,)),
        ],
        compiler_params=params,
        cost_estimate=cost("z_filter_last"),
        name="z_filter_last",
    )(passed, lines[1], lines[2], second_others, *last)


def extended(cells, sides, width):
    for axis, dim in sides:
        count = lax.axis_size(axis)
        head = lax.slice_in_dim(cells, 0, width, axis=dim)
        tail = lax.slice_in_dim(cells, cells.shape[dim] - width, cells.shape[dim], axis=dim)
        cells = jnp.concatenate(
            [
                lax.ppermute(tail, axis, [(i, (i + 1) % count) for i in range(count)]),
                cells,
                lax.ppermute(head, axis, [((i + 1) % count, i) for i in range(count)]),
            ],
            axis=dim,
        )
    return cells


def wall_zero(padded, extent, y_rows):
    height = padded.shape[1]
    all_rows = y_rows * lax.axis_size("col")
    row_index = lax.axis_index("col") * y_rows + jnp.arange(height, dtype=jnp.int32) - extent
    inside = (row_index >= 0) & (row_index < all_rows)
    return padded * inside.astype(padded.dtype)[None, :, None, None]


def shrink_rate(padded):
    center = padded[:, 1:-1, 1:-1]
    y_next = padded[:, 2:, 1:-1]
    y_prev = padded[:, :-2, 1:-1]
    z_next = padded[:, 1:-1, 2:]
    z_prev = padded[:, 1:-1, :-2]
    x_next = jnp.roll(center, -1, axis=3)
    x_prev = jnp.roll(center, 1, axis=3)
    advect = (
        center[0] * (0.5 * (x_next - x_prev))
        + center[1] * (0.5 * (y_next - y_prev))
        + center[2] * (0.5 * (z_next - z_prev))
    )
    laplace = x_next + x_prev + y_next + y_prev + z_next + z_prev - 6.0 * center
    return VISCOSITY * laplace - advect


def z_apply(received, z_filter):
    return jnp.einsum("fyos,rs->fyor", received, z_filter, preferred_element_type=jnp.float32)


def body(velocity, profile, x_filters, z_filter):
    y_rows = velocity.shape[1]

    def extend(current):
        padded = extended(current, ((("grp", "row"), 2), ("col", 1)), 1)
        return wall_zero(padded, 1, y_rows)

    section_one = velocity + STEP_SIZE * shrink_rate(extend(velocity))
    section_two = 0.75 * velocity + 0.25 * (
        section_one + STEP_SIZE * shrink_rate(extend(section_one))
    )
    advanced = velocity / 3.0 + 2.0 / 3.0 * (
        section_two + STEP_SIZE * shrink_rate(extend(section_two))
    )
    components = [advanced[0], advanced[1], advanced[2]] + [
        advanced[left_comp] * advanced[right_comp] for left_comp, right_comp in PRODUCT_PAIRS
    ]
    fields = jnp.stack(components).astype(jnp.bfloat16)
    matrices = jnp.take(x_filters, profile, axis=0)
    x_pass = jnp.einsum(
        "yox,fyzx->fyoz", matrices, fields, preferred_element_type=jnp.float32
    ).astype(jnp.bfloat16)
    filtered = z_apply(
        lax.all_to_all(x_pass, ("grp", "row"), split_axis=2, concat_axis=3, tiled=True), z_filter
    )
    stress = jnp.stack(
        [
            filtered[3 + number] - filtered[left_comp] * filtered[right_comp]
            for number, (left_comp, right_comp) in enumerate(PRODUCT_PAIRS)
        ]
    )
    return stress


def solution(mesh):
    placed = (P(None, "col", ("grp", "row"), None), P("col"), P(), P())

    def run(velocity, profile, x_filters, z_filter):
        shape = dict(mesh.shape)
        plane = shape["grp"] * shape["row"]
        suits = (
            (shape["grp"], shape["row"], shape["col"]) == (4, 2, 4)
            and velocity.shape == (3, shape["col"], 128 * plane, 1024)
            and x_filters.shape[1:] == z_filter.shape == (1024, 1024)
        )
        return jax.shard_map(
            fast_body if suits else body,
            mesh=mesh,
            in_specs=placed,
            out_specs=P(None, "col", ("grp", "row"), None),
            check_vma=False,
        )(velocity, profile, x_filters, z_filter)

    return run
```

```python
import functools

import jax
import jax.numpy as jnp
from jax import lax
from jax.experimental import pallas as pl
from jax.experimental.pallas import tpu as pltpu
from jax.sharding import PartitionSpec as P

STEP_SIZE = 0.25
VISCOSITY = 0.8
PRODUCT_PAIRS = ((0, 0), (0, 1), (0, 2), (1, 1), (1, 2), (2, 2))
FIELDS = 3 + len(PRODUCT_PAIRS)

PLANE = ("grp", "row")
WIRE = jnp.bfloat16
CHUNKS = ((0,), (1, 2), (3,))
CHIPS = (0, 1, 4, 5)
HALO = 8
REACH = 3
VMEM_BYTES = 32 * 1024 * 1024
NT = (((1,), (1,)), ((), ()))
TN = (((0,), (0,)), ((), ()))
TAIL_PARTS = 2
WAITED = 3
COSTS = dict(prepare=3.0, advance=5.0, x_filter_0=0.1, x_filter_1=0.1, x_filter_2=0.1, x_filter_3=0.1, z_filter_first=0.1, z_filter_last=0.1)


def cost(name):
    return pl.CostEstimate(flops=0, bytes_accessed=int(3.7e6 * COSTS[name]), transcendentals=0)


def exchange(value, axis, flip):
    count = lax.axis_size(axis)
    return lax.ppermute(value, axis, [(i, i ^ flip) for i in range(count)])


def delayed(value, *earlier):
    return lax.optimization_barrier((value, earlier))[0]


def whole(memory=pltpu.VMEM):
    return pl.BlockSpec(memory_space=memory)


def x_rows_kernel(place_ref, x_filters, rows_out, sem):
    me, prof = place_ref[1], place_ref[2]
    copies = []
    for core in range(2):
        for slot, flip in enumerate(CHIPS):
            number = core * len(CHIPS) + slot
            at = pl.multiple_of((me ^ flip ^ (2 * core)) * 128, 128)
            copies.append(
                pltpu.make_async_copy(
                    x_filters.at[prof, pl.ds(at, 128)], rows_out.at[pl.ds(number * 128, 128)], sem.at[number]
                )
            )
            copies[-1].start()
    for copy in copies:
        copy.wait()


def z_lines_kernel(slabs, place_ref, z_filter, *lines_out):
    q, me = place_ref[0], place_ref[1]
    rows = 128 // slabs
    target = lax.broadcasted_iota(jnp.int32, (128, 128), 0)
    source = lax.broadcasted_iota(jnp.int32, (128, 128), 1)
    pick = (source == rows * (q ^ (target // rows)) + target % rows).astype(jnp.bfloat16)
    for slot, flip in enumerate(CHIPS):
        for core in range(2):
            lanes = pl.ds(pl.multiple_of(128 * (me ^ flip ^ (2 * core)), 128), 128)
            picked = lax.dot_general(pick, z_filter[:, lanes], NT, preferred_element_type=jnp.float32)
            for number, flips in enumerate(CHUNKS):
                cells = rows * len(flips)
                part = picked[rows * flips[0] : rows * flips[0] + cells].astype(jnp.bfloat16)
                if number < len(CHUNKS) - 1:
                    at = (core * len(CHIPS) + slot) * cells
                else:
                    at = (slot * 2 + core) * cells
                lines_out[number][at : at + cells] = part


def edge_kernel(slabs, q_ref, velocity, own, tail, head, *refs):
    halos, (cells, line, sem) = refs[:slabs], refs[slabs:]
    q = q_ref[0]
    block, width = cells.shape[1:]
    rows = block // slabs
    copies = [pltpu.make_async_copy(velocity.at[comp, 0], cells.at[comp], sem.at[comp]) for comp in range(3)]
    for copy in copies:
        copy.start()

    def lay(comp, before, after):
        last = cells[comp, pl.ds(pl.multiple_of(before, HALO), HALO)][HALO - REACH :]
        first = cells[comp, pl.ds(pl.multiple_of(after, HALO), HALO)][:REACH]
        for part in range(8):
            lanes = slice(width // 8 * part, width // 8 * (part + 1))
            line[pl.ds(part, REACH, stride=8)] = last[:, lanes]
            line[pl.ds(8 * REACH + part, REACH, stride=8)] = first[:, lanes]

    for comp in range(3):
        copies[comp].wait()
        own[comp] = cells[comp, pl.ds(pl.multiple_of(rows * q, rows), rows)]
        lay(comp, block - HALO, 0)
        tail[comp] = line[: 8 * REACH].astype(WIRE)
        head[comp] = line[8 * REACH :].astype(WIRE)
        for flip in range(slabs):
            at = rows * (q ^ flip)
            lay(comp, jnp.maximum(at - HALO, 0), jnp.minimum(at + rows, block - HALO))
            halos[flip][comp] = line[...].astype(WIRE)


def step_kernel(slabs, q_ref, *refs):
    mains, halos = refs[:slabs], refs[slabs : 2 * slabs]
    outs, (start, one, two, done) = refs[2 * slabs : -4], refs[-4:]
    q = q_ref[0]
    rows, width = outs[0].shape[-2:]
    parts = width // 128
    for buffer in (start, one, two):
        buffer[0] = jnp.zeros(buffer.shape[1:], buffer.dtype)
        buffer[slabs + 1] = jnp.zeros(buffer.shape[1:], buffer.dtype)
    for flip in range(slabs):
        y = (q ^ flip) + 1
        for comp in range(3):
            for row in range(0, rows, 16):
                block = mains[flip][comp, row : row + 16].astype(jnp.float32)
                for half in range(2):
                    for part in range(parts):
                        at = (REACH + row + 8 * half) * 8 + part
                        start[y, comp, pl.ds(at, 8, stride=8)] = block[
                            8 * half : 8 * half + 8, 128 * part : 128 * part + 128
                        ]
            halo = halos[flip][comp].astype(jnp.float32)
            start[y, comp, : 8 * REACH] = halo[: 8 * REACH]
            start[y, comp, 8 * (REACH + rows) :] = halo[8 * REACH :]

    lane = lax.broadcasted_iota(jnp.int32, (8, 128), 1)
    at_end, at_start = lane == 127, lane == 0

    def sweep(src, y, first, count, emit):
        behind = [src[y, comp, 8 * first - 8 : 8 * first] for comp in range(3)]
        here = [src[y, comp, 8 * first : 8 * first + 8] for comp in range(3)]
        for row in range(first, first + count):
            ahead = [src[y, comp, 8 * row + 8 : 8 * row + 16] for comp in range(3)]
            lower, upper = [], []
            for comp in range(3):
                drift = (0.5 * STEP_SIZE) * here[comp]
                upper.append(STEP_SIZE * VISCOSITY - drift)
                lower.append(STEP_SIZE * VISCOSITY + drift)
            for comp in range(3):
                center = here[comp]
                next_lane = pltpu.roll(center, 127, 1)
                x_next = jnp.where(at_end, pltpu.roll(next_lane, 7, 0), next_lane)
                prev_lane = pltpu.roll(center, 1, 1)
                x_prev = jnp.where(at_start, pltpu.roll(prev_lane, 1, 0), prev_lane)
                y_next = src[y + 1, comp, 8 * row : 8 * row + 8]
                y_prev = src[y - 1, comp, 8 * row : 8 * row + 8]
                along_x = upper[0] * x_next + lower[0] * x_prev
                along_y = upper[1] * y_next + lower[1] * y_prev
                along_z = upper[2] * ahead[comp] + lower[2] * behind[comp]
                rest = (1.0 - 6.0 * STEP_SIZE * VISCOSITY) * center
                emit(row, comp, (along_x + along_y) + (along_z + rest))
            behind, here = here, ahead

    def section_one(number, carry):
        y = number + 1

        def emit(row, comp, moved):
            one[y, comp, 8 * row : 8 * row + 8] = moved

        sweep(start, y, 1, rows + 2 * REACH - 2, emit)
        return carry

    def section_two(number, carry):
        y = number + 1

        def emit(row, comp, moved):
            at = slice(8 * row, 8 * row + 8)
            two[y, comp, at] = 0.75 * start[y, comp, at] + 0.25 * moved

        sweep(one, y, 2, rows + 2 * REACH - 4, emit)
        return carry

    def section_three(number, carry):
        y = number + 1

        def emit(row, comp, moved):
            at = slice(8 * row, 8 * row + 8)
            to = slice(8 * (row - REACH), 8 * (row - REACH) + 8)
            done[number, comp, to] = (1.0 / 3.0) * start[y, comp, at] + (2.0 / 3.0) * moved

        sweep(two, y, REACH, rows, emit)
        return carry

    lax.fori_loop(0, slabs, section_one, 0)
    lax.fori_loop(0, slabs, section_two, 0)
    lax.fori_loop(0, slabs, section_three, 0)
    for flip in range(slabs):
        for comp in range(3):
            for row in range(0, rows, 16):
                for part in range(parts):
                    pair = [done[q ^ flip, comp, pl.ds((row + at) * 8 + part, 8, stride=8)] for at in (0, 8)]
                    outs[flip][comp, row : row + 16, 128 * part : 128 * part + 128] = jnp.concatenate(
                        pair, axis=0
                    ).astype(outs[flip].dtype)


def advance(velocity, filters):
    slabs, plane = lax.axis_size("col"), lax.axis_size(PLANE)
    q = lax.axis_index("col").astype(jnp.int32)
    v = velocity[:, 0]
    block, width = v.shape[1:]
    rows = block // slabs
    slabs_sent = [lax.dynamic_slice_in_dim(v, rows * (q ^ flip), rows, 1).astype(WIRE) for flip in range(1, slabs)]
    edge = jax.ShapeDtypeStruct((3, 8 * REACH, width // 8), WIRE)
    around = jax.ShapeDtypeStruct((3, 16 * REACH, width // 8), WIRE)
    own, tail, head, *halos = pl.pallas_call(
        functools.partial(edge_kernel, slabs),
        out_shape=[jax.ShapeDtypeStruct((3, rows, width), v.dtype), edge, edge] + [around] * slabs,
        in_specs=[whole(pltpu.SMEM), whole(pl.ANY)],
        out_specs=[whole()] * (3 + slabs),
        scratch_shapes=[
            pltpu.VMEM((3, block, width), v.dtype),
            pltpu.VMEM((16 * REACH, width // 8), v.dtype),
            pltpu.SemaphoreType.DMA((3,)),
        ],
        compiler_params=pltpu.CompilerParams(vmem_limit_bytes=VMEM_BYTES),
        cost_estimate=cost("prepare"),
        name="edges",
    )(delayed(q.reshape(1), *slabs_sent), velocity)
    tail = lax.ppermute(tail, PLANE, [(j, (j + 1) % plane) for j in range(plane)])
    head = lax.ppermute(head, PLANE, [((j + 1) % plane, j) for j in range(plane)])
    mains = [own] + [exchange(slabs_sent[flip - 1], "col", flip) for flip in range(1, slabs)]
    outer = jnp.concatenate([tail, head], axis=1)
    before = lax.broadcasted_iota(jnp.int32, around.shape, 1) < 8 * REACH
    for flip in range(slabs):
        at = rows * (q ^ flip)
        outside = jnp.logical_or(jnp.logical_and(before, at == 0), jnp.logical_and(~before, at == block - rows))
        halos[flip] = jnp.where(outside, outer, halos[flip])
    halos[1], mains[1] = lax.optimization_barrier((halos[1], mains[1]))
    for flip in (3, 2, 1):
        halos[flip] = exchange(halos[flip], "col", flip)
    mains, halos, filters = lax.optimization_barrier((mains, halos, filters))

    lines = 8 * (rows + 2 * REACH)
    pieces = pl.pallas_call(
        functools.partial(step_kernel, slabs),
        out_shape=[jax.ShapeDtypeStruct((3, rows, width), WIRE)] * slabs,
        in_specs=[whole(pltpu.SMEM)] + [whole()] * (2 * slabs),
        out_specs=[whole()] * slabs,
        scratch_shapes=[pltpu.VMEM((slabs + 2, 3, lines, 128), jnp.float32)] * 3
        + [pltpu.VMEM((slabs, 3, 8 * rows, 128), jnp.float32)],
        compiler_params=pltpu.CompilerParams(vmem_limit_bytes=VMEM_BYTES),
        cost_estimate=cost("advance"),
        name="advance",
    )(q.reshape(1), *mains, *halos)
    pieces = list(pieces)
    pieces[1], pieces[2] = exchange(pieces[1], "col", 1), exchange(pieces[2], "col", 2)
    pieces[3] = exchange(pieces[3], "col", 3)
    return pieces, filters


def x_kernel(cores, matrix, *refs):
    inputs, outs, (fields,) = refs[: -len(CHIPS) - 1], refs[-len(CHIPS) - 1 : -1], refs[-1:]
    cells = fields.shape[1]
    rows = cells // len(inputs)
    for piece, ref in enumerate(inputs):
        at = slice(rows * piece, rows * piece + rows)
        for comp in range(3):
            fields[comp, at] = ref[comp]
        for number, (a, b) in enumerate(PRODUCT_PAIRS):
            product = ref[a].astype(jnp.float32) * ref[b].astype(jnp.float32)
            fields[3 + number, at] = product.astype(jnp.bfloat16)
    group = fields[...].reshape(FIELDS * cells, fields.shape[2])
    result = lax.dot_general(
        group, matrix[: cores * len(CHIPS) * 128], NT, preferred_element_type=jnp.float32
    ).astype(jnp.bfloat16)
    for number in range(FIELDS):
        for core in range(cores):
            for slot in range(len(CHIPS)):
                at = (core * len(CHIPS) + slot) * 128
                outs[slot][core, number] = result[number * cells : (number + 1) * cells, at : at + 128]


def side_by_side(block):
    return jnp.concatenate([block[number] for number in range(FIELDS)], axis=1)


def z_sum(lines, blocks, columns):
    left = jnp.concatenate(blocks, axis=0)
    right = jnp.concatenate([line[:, columns] for line in lines], axis=0)
    return lax.dot_general(left, right, TN, preferred_element_type=jnp.float32)


def z_first_kernel(*refs):
    lines, first, others, second, passed = refs[:2], refs[2:6], refs[6], refs[7:11], refs[11]
    blocks = [side_by_side(ref[0]) for ref in first]
    blocks += [side_by_side(others[slot]) for slot in range(len(CHIPS))]
    blocks += [side_by_side(ref[0]) for ref in second]
    half = lines[1].shape[0] // 2
    passed[...] = z_sum([lines[0], lines[1].at[:half]], blocks, slice(None)).reshape(passed.shape)


def z_last_kernel(passed, line_second, line_last, others, *refs):
    blocks = [side_by_side(others[slot]) for slot in range(len(CHIPS))]
    blocks += [side_by_side(ref[0]) for ref in refs[: len(CHIPS)]]
    half = line_second.shape[0] // 2
    lines = [line_second.at[half:], line_last]
    stress, made, sem = refs[len(CHIPS) :]
    copies = []
    width = passed.shape[2] // TAIL_PARTS
    for part in range(TAIL_PARTS):
        columns = slice(part * width, (part + 1) * width)
        result = z_sum(lines, blocks, columns)
        total = [passed[at, :, columns] + result[at * 128 : (at + 1) * 128] for at in range(FIELDS)]
        for at, (a, b) in enumerate(PRODUCT_PAIRS):
            made[at, :, columns] = total[3 + at] - total[a] * total[b]
        copies.append(pltpu.make_async_copy(made.at[:, :, columns], stress.at[:, 0, :, columns], sem.at[part]))
        copies[-1].start()
    for copy in copies:
        copy.wait()


def fast_body(velocity, profile, x_filters, z_filter):
    width = velocity.shape[3]
    slabs = lax.axis_size("col")
    q = lax.axis_index("col").astype(jnp.int32)
    me = lax.axis_index(PLANE).astype(jnp.int32)
    place = jnp.stack([q, me, profile[0]])
    params = pltpu.CompilerParams(vmem_limit_bytes=VMEM_BYTES)
    sizes = [len(flips) * 128 // slabs for flips in CHUNKS]
    matrix = pl.pallas_call(
        x_rows_kernel,
        out_shape=jax.ShapeDtypeStruct((256 * len(CHIPS), width), jnp.bfloat16),
        in_specs=[whole(pltpu.SMEM), whole(pl.ANY)],
        out_specs=whole(),
        scratch_shapes=[pltpu.SemaphoreType.DMA((2 * len(CHIPS),))],
        compiler_params=params,
        cost_estimate=cost("prepare"),
        name="x_rows",
    )(place, x_filters)
    lines = pl.pallas_call(
        functools.partial(z_lines_kernel, slabs),
        out_shape=[
            jax.ShapeDtypeStruct((2 * len(CHIPS) * cells, z_filter.shape[0]), jnp.bfloat16) for cells in sizes
        ],
        in_specs=[whole(pltpu.SMEM), whole()],
        out_specs=[whole()] * len(CHUNKS),
        compiler_params=params,
        cost_estimate=cost("prepare"),
        name="z_lines",
    )(place, z_filter)

    pieces, matrix = advance(velocity, matrix)

    def x_filter(number, cores, inputs):
        cells = sum(piece.shape[1] for piece in inputs)
        return list(
            pl.pallas_call(
                functools.partial(x_kernel, cores),
                out_shape=[jax.ShapeDtypeStruct((cores, FIELDS, cells, 128), jnp.bfloat16)] * len(CHIPS),
                in_specs=[whole()] * (1 + len(inputs)),
                out_specs=[whole()] * len(CHIPS),
                scratch_shapes=[pltpu.VMEM((FIELDS, cells, width), jnp.bfloat16)],
                compiler_params=params,
                cost_estimate=cost(f"x_filter_{number}"),
                name=f"x_filter_{number}",
            )(matrix, *inputs)
        )

    def to_chips(made):
        return [made[0]] + [exchange(made[slot], PLANE, CHIPS[slot]) for slot in range(1, len(CHIPS))]

    blocks = []
    for number, flips in enumerate(CHUNKS[:-1]):
        made = x_filter(number, 2, [pieces[flip] for flip in flips])
        if blocks:
            made = delayed(made, *blocks[-1][1 : len(CHIPS)])
        sent = to_chips(made)
        blocks.append(sent)
    mine = [pieces[flip] for flip in CHUNKS[-1]]
    made = x_filter(len(CHUNKS) - 1, 1, mine + [exchange(piece, "grp", 1) for piece in mine])
    made[3] = delayed(made[3], blocks[-1][1])
    last = to_chips(made)
    first, second = blocks
    first_others = exchange(jnp.stack([block[1] for block in first]), "grp", 1)
    passed = pl.pallas_call(
        z_first_kernel,
        out_shape=jax.ShapeDtypeStruct((FIELDS, 128, width), jnp.float32),
        in_specs=[whole()] * (3 + 2 * len(CHIPS)),
        out_specs=whole(),
        compiler_params=params,
        cost_estimate=cost("z_filter_first"),
        name="z_filter_first",
    )(*lines[:2], *first, first_others, *second)
    second_others = exchange(delayed(jnp.stack([block[1] for block in second]), passed, *last[1:]), "grp", 1)
    return pl.pallas_call(
        z_last_kernel,
        out_shape=jax.ShapeDtypeStruct((len(PRODUCT_PAIRS), 1, 128, width), jnp.float32),
        in_specs=[whole()] * (4 + len(CHIPS)),
        out_specs=whole(pl.ANY),
        scratch_shapes=[
            pltpu.VMEM((len(PRODUCT_PAIRS), 128, width), jnp.float32),
            pltpu.SemaphoreType.DMA((TAIL_PARTS,)),
        ],
        compiler_params=params,
        cost_estimate=cost("z_filter_last"),
        name="z_filter_last",
    )(passed, lines[1], lines[2], second_others, *last)


def extended(cells, sides, width):
    for axis, dim in sides:
        count = lax.axis_size(axis)
        head = lax.slice_in_dim(cells, 0, width, axis=dim)
        tail = lax.slice_in_dim(cells, cells.shape[dim] - width, cells.shape[dim], axis=dim)
        cells = jnp.concatenate(
            [
                lax.ppermute(tail, axis, [(i, (i + 1) % count) for i in range(count)]),
                cells,
                lax.ppermute(head, axis, [((i + 1) % count, i) for i in range(count)]),
            ],
            axis=dim,
        )
    return cells


def wall_zero(padded, extent, y_rows):
    height = padded.shape[1]
    all_rows = y_rows * lax.axis_size("col")
    row_index = lax.axis_index("col") * y_rows + jnp.arange(height, dtype=jnp.int32) - extent
    inside = (row_index >= 0) & (row_index < all_rows)
    return padded * inside.astype(padded.dtype)[None, :, None, None]


def shrink_rate(padded):
    center = padded[:, 1:-1, 1:-1]
    y_next = padded[:, 2:, 1:-1]
    y_prev = padded[:, :-2, 1:-1]
    z_next = padded[:, 1:-1, 2:]
    z_prev = padded[:, 1:-1, :-2]
    x_next = jnp.roll(center, -1, axis=3)
    x_prev = jnp.roll(center, 1, axis=3)
    advect = (
        center[0] * (0.5 * (x_next - x_prev))
        + center[1] * (0.5 * (y_next - y_prev))
        + center[2] * (0.5 * (z_next - z_prev))
    )
    laplace = x_next + x_prev + y_next + y_prev + z_next + z_prev - 6.0 * center
    return VISCOSITY * laplace - advect


def z_apply(received, z_filter):
    return jnp.einsum("fyos,rs->fyor", received, z_filter, preferred_element_type=jnp.float32)


def body(velocity, profile, x_filters, z_filter):
    y_rows = velocity.shape[1]

    def extend(current):
        padded = extended(current, ((("grp", "row"), 2), ("col", 1)), 1)
        return wall_zero(padded, 1, y_rows)

    section_one = velocity + STEP_SIZE * shrink_rate(extend(velocity))
    section_two = 0.75 * velocity + 0.25 * (
        section_one + STEP_SIZE * shrink_rate(extend(section_one))
    )
    advanced = velocity / 3.0 + 2.0 / 3.0 * (
        section_two + STEP_SIZE * shrink_rate(extend(section_two))
    )
    components = [advanced[0], advanced[1], advanced[2]] + [
        advanced[left_comp] * advanced[right_comp] for left_comp, right_comp in PRODUCT_PAIRS
    ]
    fields = jnp.stack(components).astype(jnp.bfloat16)
    matrices = jnp.take(x_filters, profile, axis=0)
    x_pass = jnp.einsum(
        "yox,fyzx->fyoz", matrices, fields, preferred_element_type=jnp.float32
    ).astype(jnp.bfloat16)
    filtered = z_apply(
        lax.all_to_all(x_pass, ("grp", "row"), split_axis=2, concat_axis=3, tiled=True), z_filter
    )
    stress = jnp.stack(
        [
            filtered[3 + number] - filtered[left_comp] * filtered[right_comp]
            for number, (left_comp, right_comp) in enumerate(PRODUCT_PAIRS)
        ]
    )
    return stress


def solution(mesh):
    placed = (P(None, "col", ("grp", "row"), None), P("col"), P(), P())

    def run(velocity, profile, x_filters, z_filter):
        shape = dict(mesh.shape)
        plane = shape["grp"] * shape["row"]
        suits = (
            (shape["grp"], shape["row"], shape["col"]) == (4, 2, 4)
            and velocity.shape == (3, shape["col"], 128 * plane, 1024)
            and x_filters.shape[1:] == z_filter.shape == (1024, 1024)
        )
        return jax.shard_map(
            fast_body if suits else body,
            mesh=mesh,
            in_specs=placed,
            out_specs=P(None, "col", ("grp", "row"), None),
            check_vma=False,
        )(velocity, profile, x_filters, z_filter)

    return run
```

```python
import functools

import jax
import jax.numpy as jnp
from jax import lax
from jax.experimental import pallas as pl
from jax.experimental.pallas import tpu as pltpu
from jax.sharding import PartitionSpec as P

STEP_SIZE = 0.25
VISCOSITY = 0.8
PRODUCT_PAIRS = ((0, 0), (0, 1), (0, 2), (1, 1), (1, 2), (2, 2))
FIELDS = 3 + len(PRODUCT_PAIRS)

PLANE = ("grp", "row")
WIRE = jnp.bfloat16
CHUNKS = ((0,), (1, 2), (3,))
CHIPS = (0, 1, 4, 5)
HALO = 8
REACH = 3
VMEM_BYTES = 32 * 1024 * 1024
NT = (((1,), (1,)), ((), ()))
TN = (((0,), (0,)), ((), ()))
TAIL_PARTS = 2
WAITED = 3
COSTS = dict(prepare=3.0, advance=5.0, x_filter_0=0.1, x_filter_1=0.1, x_filter_2=0.1, x_filter_3=0.1, z_filter_first=0.1, z_filter_last=0.1)


def cost(name):
    return pl.CostEstimate(flops=0, bytes_accessed=int(3.7e6 * COSTS[name]), transcendentals=0)


def exchange(value, axis, flip):
    count = lax.axis_size(axis)
    return lax.ppermute(value, axis, [(i, i ^ flip) for i in range(count)])


def delayed(value, *earlier):
    return lax.optimization_barrier((value, earlier))[0]


def whole(memory=pltpu.VMEM):
    return pl.BlockSpec(memory_space=memory)


def x_rows_kernel(place_ref, x_filters, rows_out, sem):
    me, prof = place_ref[1], place_ref[2]
    copies = []
    for core in range(2):
        for slot, flip in enumerate(CHIPS):
            number = core * len(CHIPS) + slot
            at = pl.multiple_of((me ^ flip ^ (2 * core)) * 128, 128)
            copies.append(
                pltpu.make_async_copy(
                    x_filters.at[prof, pl.ds(at, 128)], rows_out.at[pl.ds(number * 128, 128)], sem.at[number]
                )
            )
            copies[-1].start()
    for copy in copies:
        copy.wait()


def z_lines_kernel(slabs, place_ref, z_filter, *lines_out):
    q, me = place_ref[0], place_ref[1]
    rows = 128 // slabs
    target = lax.broadcasted_iota(jnp.int32, (128, 128), 0)
    source = lax.broadcasted_iota(jnp.int32, (128, 128), 1)
    pick = (source == rows * (q ^ (target // rows)) + target % rows).astype(jnp.bfloat16)
    for slot, flip in enumerate(CHIPS):
        for core in range(2):
            lanes = pl.ds(pl.multiple_of(128 * (me ^ flip ^ (2 * core)), 128), 128)
            picked = lax.dot_general(pick, z_filter[:, lanes], NT, preferred_element_type=jnp.float32)
            for number, flips in enumerate(CHUNKS):
                cells = rows * len(flips)
                part = picked[rows * flips[0] : rows * flips[0] + cells].astype(jnp.bfloat16)
                if number < len(CHUNKS) - 1:
                    at = (core * len(CHIPS) + slot) * cells
                else:
                    at = (slot * 2 + core) * cells
                lines_out[number][at : at + cells] = part


def edge_kernel(slabs, q_ref, velocity, own, tail, head, *refs):
    halos, (cells, line, sem) = refs[:slabs], refs[slabs:]
    q = q_ref[0]
    block, width = cells.shape[1:]
    rows = block // slabs
    copies = [pltpu.make_async_copy(velocity.at[comp, 0], cells.at[comp], sem.at[comp]) for comp in range(3)]
    for copy in copies:
        copy.start()

    def lay(comp, before, after):
        last = cells[comp, pl.ds(pl.multiple_of(before, HALO), HALO)][HALO - REACH :]
        first = cells[comp, pl.ds(pl.multiple_of(after, HALO), HALO)][:REACH]
        for part in range(8):
            lanes = slice(width // 8 * part, width // 8 * (part + 1))
            line[pl.ds(part, REACH, stride=8)] = last[:, lanes]
            line[pl.ds(8 * REACH + part, REACH, stride=8)] = first[:, lanes]

    for comp in range(3):
        copies[comp].wait()
        own[comp] = cells[comp, pl.ds(pl.multiple_of(rows * q, rows), rows)]
        lay(comp, block - HALO, 0)
        tail[comp] = line[: 8 * REACH].astype(WIRE)
        head[comp] = line[8 * REACH : 16 * REACH].astype(WIRE)
        for flip in range(slabs):
            at = rows * (q ^ flip)
            lay(comp, jnp.maximum(at - HALO, 0), jnp.minimum(at + rows, block - HALO))
            halos[flip][comp] = line[: 16 * REACH].astype(WIRE)


def step_kernel(slabs, q_ref, *refs):
    mains, halos = refs[:slabs], refs[slabs : 2 * slabs]
    outs, (start, one, two, done) = refs[2 * slabs : -4], refs[-4:]
    q = q_ref[0]
    rows, width = outs[0].shape[-2:]
    parts = width // 128
    for buffer in (start, one, two):
        buffer[0] = jnp.zeros(buffer.shape[1:], buffer.dtype)
        buffer[slabs + 1] = jnp.zeros(buffer.shape[1:], buffer.dtype)
    for flip in range(slabs):
        y = (q ^ flip) + 1
        for comp in range(3):
            for row in range(0, rows, 16):
                block = mains[flip][comp, row : row + 16].astype(jnp.float32)
                for half in range(2):
                    for part in range(parts):
                        at = (REACH + row + 8 * half) * 8 + part
                        start[y, comp, pl.ds(at, 8, stride=8)] = block[
                            8 * half : 8 * half + 8, 128 * part : 128 * part + 128
                        ]
            halo = halos[flip][comp].astype(jnp.float32)
            start[y, comp, : 8 * REACH] = halo[: 8 * REACH]
            start[y, comp, 8 * (REACH + rows) :] = halo[8 * REACH :]

    lane = lax.broadcasted_iota(jnp.int32, (8, 128), 1)
    at_end, at_start = lane == 127, lane == 0

    def sweep(src, y, first, count, emit):
        behind = [src[y, comp, 8 * first - 8 : 8 * first] for comp in range(3)]
        here = [src[y, comp, 8 * first : 8 * first + 8] for comp in range(3)]
        for row in range(first, first + count):
            ahead = [src[y, comp, 8 * row + 8 : 8 * row + 16] for comp in range(3)]
            lower, upper = [], []
            for comp in range(3):
                drift = (0.5 * STEP_SIZE) * here[comp]
                upper.append(STEP_SIZE * VISCOSITY - drift)
                lower.append(STEP_SIZE * VISCOSITY + drift)
            for comp in range(3):
                center = here[comp]
                next_lane = pltpu.roll(center, 127, 1)
                x_next = jnp.where(at_end, pltpu.roll(next_lane, 7, 0), next_lane)
                prev_lane = pltpu.roll(center, 1, 1)
                x_prev = jnp.where(at_start, pltpu.roll(prev_lane, 1, 0), prev_lane)
                y_next = src[y + 1, comp, 8 * row : 8 * row + 8]
                y_prev = src[y - 1, comp, 8 * row : 8 * row + 8]
                along_x = upper[0] * x_next + lower[0] * x_prev
                along_y = upper[1] * y_next + lower[1] * y_prev
                along_z = upper[2] * ahead[comp] + lower[2] * behind[comp]
                rest = (1.0 - 6.0 * STEP_SIZE * VISCOSITY) * center
                emit(row, comp, (along_x + along_y) + (along_z + rest))
            behind, here = here, ahead

    def section_one(number, carry):
        y = number + 1

        def emit(row, comp, moved):
            one[y, comp, 8 * row : 8 * row + 8] = moved

        sweep(start, y, 1, rows + 2 * REACH - 2, emit)
        return carry

    def section_two(number, carry):
        y = number + 1

        def emit(row, comp, moved):
            at = slice(8 * row, 8 * row + 8)
            two[y, comp, at] = 0.75 * start[y, comp, at] + 0.25 * moved

        sweep(one, y, 2, rows + 2 * REACH - 4, emit)
        return carry

    def section_three(number, carry):
        y = number + 1

        def emit(row, comp, moved):
            at = slice(8 * row, 8 * row + 8)
            to = slice(8 * (row - REACH), 8 * (row - REACH) + 8)
            done[number, comp, to] = (1.0 / 3.0) * start[y, comp, at] + (2.0 / 3.0) * moved

        sweep(two, y, REACH, rows, emit)
        return carry

    lax.fori_loop(0, slabs, section_one, 0)
    lax.fori_loop(0, slabs, section_two, 0)
    lax.fori_loop(0, slabs, section_three, 0)
    for flip in range(slabs):
        for comp in range(3):
            for row in range(0, rows, 16):
                for part in range(parts):
                    pair = [done[q ^ flip, comp, pl.ds((row + at) * 8 + part, 8, stride=8)] for at in (0, 8)]
                    outs[flip][comp, row : row + 16, 128 * part : 128 * part + 128] = jnp.concatenate(
                        pair, axis=0
                    ).astype(outs[flip].dtype)


def advance(velocity, filters):
    slabs, plane = lax.axis_size("col"), lax.axis_size(PLANE)
    q = lax.axis_index("col").astype(jnp.int32)
    v = velocity[:, 0]
    block, width = v.shape[1:]
    rows = block // slabs
    slabs_sent = [lax.dynamic_slice_in_dim(v, rows * (q ^ flip), rows, 1).astype(WIRE) for flip in range(1, slabs)]
    edge = jax.ShapeDtypeStruct((3, 8 * REACH, width // 8), WIRE)
    around = jax.ShapeDtypeStruct((3, 16 * REACH, width // 8), WIRE)
    own, tail, head, *halos = pl.pallas_call(
        functools.partial(edge_kernel, slabs),
        out_shape=[jax.ShapeDtypeStruct((3, rows, width), v.dtype), edge, edge] + [around] * slabs,
        in_specs=[whole(pltpu.SMEM), whole(pl.ANY)],
        out_specs=[whole()] * (3 + slabs),
        scratch_shapes=[
            pltpu.VMEM((3, block, width), v.dtype),
            pltpu.VMEM((16 * REACH + 64, width // 8), v.dtype),
            pltpu.SemaphoreType.DMA((3,)),
        ],
        compiler_params=pltpu.CompilerParams(vmem_limit_bytes=VMEM_BYTES),
        cost_estimate=cost("prepare"),
        name="edges",
    )(delayed(q.reshape(1), *slabs_sent), velocity)
    tail = lax.ppermute(tail, PLANE, [(j, (j + 1) % plane) for j in range(plane)])
    head = lax.ppermute(head, PLANE, [((j + 1) % plane, j) for j in range(plane)])
    mains = [own] + [exchange(slabs_sent[flip - 1], "col", flip) for flip in range(1, slabs)]
    outer = jnp.concatenate([tail, head], axis=1)
    before = lax.broadcasted_iota(jnp.int32, around.shape, 1) < 8 * REACH
    for flip in range(slabs):
        at = rows * (q ^ flip)
        outside = jnp.logical_or(jnp.logical_and(before, at == 0), jnp.logical_and(~before, at == block - rows))
        halos[flip] = jnp.where(outside, outer, halos[flip])
    halos[1], mains[1] = lax.optimization_barrier((halos[1], mains[1]))
    for flip in (3, 2, 1):
        halos[flip] = exchange(halos[flip], "col", flip)
    mains, halos, filters = lax.optimization_barrier((mains, halos, filters))

    lines = 8 * (rows + 2 * REACH)
    pieces = pl.pallas_call(
        functools.partial(step_kernel, slabs),
        out_shape=[jax.ShapeDtypeStruct((3, rows, width), WIRE)] * slabs,
        in_specs=[whole(pltpu.SMEM)] + [whole()] * (2 * slabs),
        out_specs=[whole()] * slabs,
        scratch_shapes=[pltpu.VMEM((slabs + 2, 3, lines, 128), jnp.float32)] * 3
        + [pltpu.VMEM((slabs, 3, 8 * rows, 128), jnp.float32)],
        compiler_params=pltpu.CompilerParams(vmem_limit_bytes=VMEM_BYTES),
        cost_estimate=cost("advance"),
        name="advance",
    )(q.reshape(1), *mains, *halos)
    pieces = list(pieces)
    pieces[1], pieces[2] = exchange(pieces[1], "col", 1), exchange(pieces[2], "col", 2)
    pieces[3] = exchange(pieces[3], "col", 3)
    return pieces, filters


def x_kernel(cores, matrix, *refs):
    inputs, outs, (fields,) = refs[: -len(CHIPS) - 1], refs[-len(CHIPS) - 1 : -1], refs[-1:]
    cells = fields.shape[1]
    rows = cells // len(inputs)
    for piece, ref in enumerate(inputs):
        at = slice(rows * piece, rows * piece + rows)
        for comp in range(3):
            fields[comp, at] = ref[comp]
        for number, (a, b) in enumerate(PRODUCT_PAIRS):
            product = ref[a].astype(jnp.float32) * ref[b].astype(jnp.float32)
            fields[3 + number, at] = product.astype(jnp.bfloat16)
    group = fields[...].reshape(FIELDS * cells, fields.shape[2])
    result = lax.dot_general(
        group, matrix[: cores * len(CHIPS) * 128], NT, preferred_element_type=jnp.float32
    ).astype(jnp.bfloat16)
    for number in range(FIELDS):
        for core in range(cores):
            for slot in range(len(CHIPS)):
                at = (core * len(CHIPS) + slot) * 128
                outs[slot][core, number] = result[number * cells : (number + 1) * cells, at : at + 128]


def side_by_side(block):
    return jnp.concatenate([block[number] for number in range(FIELDS)], axis=1)


def z_sum(lines, blocks, columns):
    left = jnp.concatenate(blocks, axis=0)
    right = jnp.concatenate([line[:, columns] for line in lines], axis=0)
    return lax.dot_general(left, right, TN, preferred_element_type=jnp.float32)


def z_first_kernel(*refs):
    lines, first, others, second, passed = refs[:2], refs[2:6], refs[6], refs[7:11], refs[11]
    blocks = [side_by_side(ref[0]) for ref in first]
    blocks += [side_by_side(others[slot]) for slot in range(len(CHIPS))]
    blocks += [side_by_side(ref[0]) for ref in second]
    half = lines[1].shape[0] // 2
    passed[...] = z_sum([lines[0], lines[1].at[:half]], blocks, slice(None)).reshape(passed.shape)


def z_last_kernel(passed, line_second, line_last, others, *refs):
    blocks = [side_by_side(others[slot]) for slot in range(len(CHIPS))]
    blocks += [side_by_side(ref[0]) for ref in refs[: len(CHIPS)]]
    half = line_second.shape[0] // 2
    lines = [line_second.at[half:], line_last]
    stress, made, sem = refs[len(CHIPS) :]
    copies = []
    width = passed.shape[2] // TAIL_PARTS
    for part in range(TAIL_PARTS):
        columns = slice(part * width, (part + 1) * width)
        result = z_sum(lines, blocks, columns)
        total = [passed[at, :, columns] + result[at * 128 : (at + 1) * 128] for at in range(FIELDS)]
        for at, (a, b) in enumerate(PRODUCT_PAIRS):
            made[at, :, columns] = total[3 + at] - total[a] * total[b]
        copies.append(pltpu.make_async_copy(made.at[:, :, columns], stress.at[:, 0, :, columns], sem.at[part]))
        copies[-1].start()
    for copy in copies:
        copy.wait()


def fast_body(velocity, profile, x_filters, z_filter):
    width = velocity.shape[3]
    slabs = lax.axis_size("col")
    q = lax.axis_index("col").astype(jnp.int32)
    me = lax.axis_index(PLANE).astype(jnp.int32)
    place = jnp.stack([q, me, profile[0]])
    params = pltpu.CompilerParams(vmem_limit_bytes=VMEM_BYTES)
    sizes = [len(flips) * 128 // slabs for flips in CHUNKS]
    matrix = pl.pallas_call(
        x_rows_kernel,
        out_shape=jax.ShapeDtypeStruct((256 * len(CHIPS), width), jnp.bfloat16),
        in_specs=[whole(pltpu.SMEM), whole(pl.ANY)],
        out_specs=whole(),
        scratch_shapes=[pltpu.SemaphoreType.DMA((2 * len(CHIPS),))],
        compiler_params=params,
        cost_estimate=cost("prepare"),
        name="x_rows",
    )(place, x_filters)
    lines = pl.pallas_call(
        functools.partial(z_lines_kernel, slabs),
        out_shape=[
            jax.ShapeDtypeStruct((2 * len(CHIPS) * cells, z_filter.shape[0]), jnp.bfloat16) for cells in sizes
        ],
        in_specs=[whole(pltpu.SMEM), whole()],
        out_specs=[whole()] * len(CHUNKS),
        compiler_params=params,
        cost_estimate=cost("prepare"),
        name="z_lines",
    )(place, z_filter)

    pieces, matrix = advance(velocity, matrix)

    def x_filter(number, cores, inputs):
        cells = sum(piece.shape[1] for piece in inputs)
        return list(
            pl.pallas_call(
                functools.partial(x_kernel, cores),
                out_shape=[jax.ShapeDtypeStruct((cores, FIELDS, cells, 128), jnp.bfloat16)] * len(CHIPS),
                in_specs=[whole()] * (1 + len(inputs)),
                out_specs=[whole()] * len(CHIPS),
                scratch_shapes=[pltpu.VMEM((FIELDS, cells, width), jnp.bfloat16)],
                compiler_params=params,
                cost_estimate=cost(f"x_filter_{number}"),
                name=f"x_filter_{number}",
            )(matrix, *inputs)
        )

    def to_chips(made):
        return [made[0]] + [exchange(made[slot], PLANE, CHIPS[slot]) for slot in range(1, len(CHIPS))]

    blocks = []
    for number, flips in enumerate(CHUNKS[:-1]):
        made = x_filter(number, 2, [pieces[flip] for flip in flips])
        if blocks:
            made = delayed(made, *blocks[-1][1 : len(CHIPS)])
        sent = to_chips(made)
        blocks.append(sent)
    mine = [pieces[flip] for flip in CHUNKS[-1]]
    made = x_filter(len(CHUNKS) - 1, 1, mine + [exchange(piece, "grp", 1) for piece in mine])
    made[3] = delayed(made[3], blocks[-1][1])
    last = to_chips(made)
    first, second = blocks
    first_others = exchange(jnp.stack([block[1] for block in first]), "grp", 1)
    passed = pl.pallas_call(
        z_first_kernel,
        out_shape=jax.ShapeDtypeStruct((FIELDS, 128, width), jnp.float32),
        in_specs=[whole()] * (3 + 2 * len(CHIPS)),
        out_specs=whole(),
        compiler_params=params,
        cost_estimate=cost("z_filter_first"),
        name="z_filter_first",
    )(*lines[:2], *first, first_others, *second)
    second_others = exchange(delayed(jnp.stack([block[1] for block in second]), passed, *last[1:]), "grp", 1)
    return pl.pallas_call(
        z_last_kernel,
        out_shape=jax.ShapeDtypeStruct((len(PRODUCT_PAIRS), 1, 128, width), jnp.float32),
        in_specs=[whole()] * (4 + len(CHIPS)),
        out_specs=whole(pl.ANY),
        scratch_shapes=[
            pltpu.VMEM((len(PRODUCT_PAIRS), 128, width), jnp.float32),
            pltpu.SemaphoreType.DMA((TAIL_PARTS,)),
        ],
        compiler_params=params,
        cost_estimate=cost("z_filter_last"),
        name="z_filter_last",
    )(passed, lines[1], lines[2], second_others, *last)


def extended(cells, sides, width):
    for axis, dim in sides:
        count = lax.axis_size(axis)
        head = lax.slice_in_dim(cells, 0, width, axis=dim)
        tail = lax.slice_in_dim(cells, cells.shape[dim] - width, cells.shape[dim], axis=dim)
        cells = jnp.concatenate(
            [
                lax.ppermute(tail, axis, [(i, (i + 1) % count) for i in range(count)]),
                cells,
                lax.ppermute(head, axis, [((i + 1) % count, i) for i in range(count)]),
            ],
            axis=dim,
        )
    return cells


def wall_zero(padded, extent, y_rows):
    height = padded.shape[1]
    all_rows = y_rows * lax.axis_size("col")
    row_index = lax.axis_index("col") * y_rows + jnp.arange(height, dtype=jnp.int32) - extent
    inside = (row_index >= 0) & (row_index < all_rows)
    return padded * inside.astype(padded.dtype)[None, :, None, None]


def shrink_rate(padded):
    center = padded[:, 1:-1, 1:-1]
    y_next = padded[:, 2:, 1:-1]
    y_prev = padded[:, :-2, 1:-1]
    z_next = padded[:, 1:-1, 2:]
    z_prev = padded[:, 1:-1, :-2]
    x_next = jnp.roll(center, -1, axis=3)
    x_prev = jnp.roll(center, 1, axis=3)
    advect = (
        center[0] * (0.5 * (x_next - x_prev))
        + center[1] * (0.5 * (y_next - y_prev))
        + center[2] * (0.5 * (z_next - z_prev))
    )
    laplace = x_next + x_prev + y_next + y_prev + z_next + z_prev - 6.0 * center
    return VISCOSITY * laplace - advect


def z_apply(received, z_filter):
    return jnp.einsum("fyos,rs->fyor", received, z_filter, preferred_element_type=jnp.float32)


def body(velocity, profile, x_filters, z_filter):
    y_rows = velocity.shape[1]

    def extend(current):
        padded = extended(current, ((("grp", "row"), 2), ("col", 1)), 1)
        return wall_zero(padded, 1, y_rows)

    section_one = velocity + STEP_SIZE * shrink_rate(extend(velocity))
    section_two = 0.75 * velocity + 0.25 * (
        section_one + STEP_SIZE * shrink_rate(extend(section_one))
    )
    advanced = velocity / 3.0 + 2.0 / 3.0 * (
        section_two + STEP_SIZE * shrink_rate(extend(section_two))
    )
    components = [advanced[0], advanced[1], advanced[2]] + [
        advanced[left_comp] * advanced[right_comp] for left_comp, right_comp in PRODUCT_PAIRS
    ]
    fields = jnp.stack(components).astype(jnp.bfloat16)
    matrices = jnp.take(x_filters, profile, axis=0)
    x_pass = jnp.einsum(
        "yox,fyzx->fyoz", matrices, fields, preferred_element_type=jnp.float32
    ).astype(jnp.bfloat16)
    filtered = z_apply(
        lax.all_to_all(x_pass, ("grp", "row"), split_axis=2, concat_axis=3, tiled=True), z_filter
    )
    stress = jnp.stack(
        [
            filtered[3 + number] - filtered[left_comp] * filtered[right_comp]
            for number, (left_comp, right_comp) in enumerate(PRODUCT_PAIRS)
        ]
    )
    return stress


def solution(mesh):
    placed = (P(None, "col", ("grp", "row"), None), P("col"), P(), P())

    def run(velocity, profile, x_filters, z_filter):
        shape = dict(mesh.shape)
        plane = shape["grp"] * shape["row"]
        suits = (
            (shape["grp"], shape["row"], shape["col"]) == (4, 2, 4)
            and velocity.shape == (3, shape["col"], 128 * plane, 1024)
            and x_filters.shape[1:] == z_filter.shape == (1024, 1024)
        )
        return jax.shard_map(
            fast_body if suits else body,
            mesh=mesh,
            in_specs=placed,
            out_specs=P(None, "col", ("grp", "row"), None),
            check_vma=False,
        )(velocity, profile, x_filters, z_filter)

    return run
```
